1024 devices in a mesh: dp: 64 (over z, y), fsdp: 16 (over x, core).
Axes of the slice: x: 8, y: 8, z: 8, core: 2. Of those that a mesh axis runs over, the one named last changes fastest.
Arguments:
- qkv_codes: bfloat16 [64, 16, 128, 3, 896], P('dp', 'fsdp'), may hold values from -4 to 4, as said below
- block_scales: bfloat16 [64, 16, 128, 3, 7], P('dp', 'fsdp'), may hold values from 0.25 to 2
- home_segments: int32 [64, 16, 128], P('dp', 'fsdp'), may hold values from -1 to 131, as said below
- kept_rows: int32 [64, 16], P('dp', 'fsdp'), may hold values from 32 to 64, as said below
- pack_list: int32 [64, 16, 4, 3], P(None, 'fsdp'), may hold values from 0 to 112, as said below
- w_out: bfloat16 [896, 1792], P('fsdp'), may hold values from -0.1875 to 0.1875
- cotangent: bfloat16 [64, 16, 128, 1792], P('dp', 'fsdp'), may hold values from -4 to 4
Outputs:
- output: bfloat16 [64, 16, 128, 1792], P('dp', 'fsdp')
- grad_codes: bfloat16 [64, 16, 128, 3, 896], P('dp', 'fsdp')
- grad_w_out: float32 [64, 896, 1792], P('dp', 'fsdp')
The draws below stay inside these ranges and needn't reach their ends.
Inputs may be any that keep to these rules, and one draw needn't show every extreme that they name: Rows below kept_rows are whole images or the first part of one, and stay in place; the first image of every device has at least 3 rows. `pack_list`: one table for each fsdp index, the same on all its dp devices. Entry [s, d] describes the one whole image that dp index s sends to s + offset(d), offsets +1, -1, +2, -2, always inside the axis; length 0 means none, with the other entries 0. Lengths run from 3 to 16 and reach 16. Sent images lie at or above the source's kept_rows without intersection; placed images lie at or above the target's kept_rows without intersection, below 128. `home_segments`: kept rows carry their image number, runs of equal numbers; rows of the image sent in direction d carry 128 + d; other rows -1. `qkv_codes`: every entry is a value of the e4m3 8-bit float format.
All inputs are finite; a program needn't handle non-finite values.
Results may differ from the reference program's by a relative error of at most 0.02.
Values may be sent and summed in bfloat16 or wider, within the bound.
No kernel may reach another device: no remote copies, remote signals or barrier semaphores. Data moves between devices by JAX's collectives and lax.ppermute only.
A program may use at most 32 MiB of HBM per device.

```python
import math
import jax
import jax.numpy as jnp
from jax import lax

D = 1792
HD = 112
HEADS = 8
ROWS = 128
HW = 896
NB = 7
SLOT = 16
N_DP = 64
N_FSDP = 16


def pack_tables(key):
    key_keep, key_send, key_length, key_images = jax.random.split(key, 4)
    steps_away = (1, -1, 2, -2)
    kept = jax.random.randint(key_keep, (N_DP, N_FSDP), ROWS // 4, ROWS // 2 + 1)
    kept = kept.at[0].set(ROWS // 2).at[1].set(ROWS // 4).at[2].set(ROWS // 2)
    source = jnp.arange(N_DP)[:, None, None]
    direction = jnp.arange(4)[None, None, :]
    target = source + jnp.array(steps_away, jnp.int32)[None, None, :]
    allowed = ((target >= 0) & (target < N_DP)).astype(jnp.int32)
    forced = (source == 0) & (direction == 0) | (source == 1) & (direction == 1) | (source == 0) & (direction == 2) | (source == 2)
    sending = jax.random.randint(key_send, (N_DP, N_FSDP, 4), 0, 2)
    sending = jnp.where(forced, 1, sending) * allowed
    length = jax.random.randint(key_length, (N_DP, N_FSDP, 4), 3, SLOT + 1)
    full_slot = (source == 0) & (direction == 0) | (source == 2) & (direction < 3)
    length = jnp.where(full_slot, SLOT, length) * sending
    home_start = kept[:, :, None] + jnp.cumsum(length, axis=-1) - length
    arriving = jnp.stack([jnp.roll(length[:, :, route], steps_away[route], axis=0) for route in range(4)], axis=-1)
    placed = kept[:, :, None] + jnp.cumsum(arriving, axis=-1) - arriving
    landing = jnp.stack([jnp.roll(placed[:, :, route], -steps_away[route], axis=0) for route in range(4)], axis=-1)
    present = length > 0
    table = jnp.stack([jnp.where(present, home_start, 0), length, jnp.where(present, landing, 0)], axis=-1)
    row_index = jnp.arange(ROWS)[None, None, :]
    starts = (jax.random.randint(key_images, (N_DP, N_FSDP, ROWS), 0, 12) == 0) & (row_index >= 3)
    image_ids = jnp.cumsum(starts.astype(jnp.int32), axis=-1)
    home_ids = jnp.where(row_index < kept[:, :, None], image_ids, -1)
    for route in range(4):
        begin_row = home_start[:, :, route:route + 1]
        inside = (row_index >= begin_row) & (row_index < begin_row + length[:, :, route:route + 1])
        home_ids = jnp.where(inside, ROWS + route, home_ids)
    return (kept.astype(jnp.int32), table.astype(jnp.int32), home_ids.astype(jnp.int32))


def draw_kept_rows(key, part):
    tables = pack_tables(key)
    return tables[0]


def draw_pack_list(key, part):
    tables = pack_tables(key)
    return tables[1]


def draw_home_segments(key, part):
    tables = pack_tables(key)
    return tables[2]


def small_code(sign_bits, power_index, mantissa):
    powers = jnp.array([0.125, 0.25, 0.5, 1.0, 2.0], jnp.float32)
    signs = 2.0 * sign_bits.astype(jnp.float32) - 1.0
    return signs * powers[power_index] * (1.0 + mantissa.astype(jnp.float32) / 8.0)


def draw_qkv_codes(key, part):
    key = jax.random.fold_in(key, 11)
    shape = (N_DP, N_FSDP, ROWS, 3, HW)
    key_sign, key_first, key_second, key_mant = jax.random.split(key, 4)
    sign_bits = jax.random.randint(key_sign, shape, 0, 2)
    mantissa = jax.random.randint(key_mant, shape, 0, 8)
    power_index = jax.random.randint(key_first, shape, 0, 3) + jax.random.randint(key_second, shape, 0, 3)
    codes = small_code(sign_bits, power_index, mantissa)
    return codes.astype(jnp.bfloat16)


def draw_block_scales(key, part):
    key = jax.random.fold_in(key, 12)
    shape = (N_DP, N_FSDP, ROWS, 3, NB)
    scales = jnp.exp(jax.random.uniform(key, shape, jnp.float32, jnp.log(0.25), jnp.log(2.0)))
    return scales.astype(jnp.bfloat16)


def levels(key, shape, pieces, low, largest):
    factor_of = 1.0
    for dim, parts in pieces:
        heights = jax.random.uniform(jax.random.fold_in(jax.random.fold_in(key, 6), dim), (parts,), jnp.float32, low / len(pieces), largest / len(pieces))
        factor_of = factor_of * jnp.repeat(jnp.exp(heights), shape[dim] // parts).reshape((-1,) + (1,) * (len(shape) - 1 - dim))
    return factor_of


def noise(key, extent, deviation, limit, cuts=(), kind=jnp.bfloat16):
    values = deviation * jax.random.normal(key, extent, jnp.float32)
    if cuts:
        values = values * levels(key, extent, cuts, -0.22, 0.18)
    return jnp.clip(values, -limit, limit).astype(kind)


def setup_inputs(seed: int = 0) -> dict:
    key_list = jax.random.split(jax.random.key(seed), 8)
    qkv_codes = draw_qkv_codes(jax.random.fold_in(key_list[7], 71), 0)
    block_scales = draw_block_scales(jax.random.fold_in(key_list[7], 71), 0)
    home_segments = draw_home_segments(jax.random.fold_in(key_list[7], 71), 0)
    kept_rows = draw_kept_rows(jax.random.fold_in(key_list[7], 71), 0)
    pack_list = draw_pack_list(jax.random.fold_in(key_list[7], 71), 0)
    w_out = noise(key_list[5], (HW, D), HW ** -0.5, 0.1875, ((0, 16),))
    cotangent = noise(key_list[6], (N_DP, N_FSDP, ROWS, D), 0.25, 4.0, ((0, 64), (1, 16)))
    return {"qkv_codes": qkv_codes, "block_scales": block_scales, "home_segments": home_segments, "kept_rows": kept_rows, "pack_list": pack_list, "w_out": w_out, "cotangent": cotangent}


offsets = (1, -1, 2, -2)

def dequantize(codes, scales):
    count = codes.shape[0]
    blocks = scales.shape[-1]
    scaled = codes.astype(jnp.float32).reshape(count, 3, blocks, -1) * scales.astype(jnp.float32)[..., None]
    return scaled.reshape(count, 3, -1).astype(jnp.bfloat16)

def local_layer(codes, scales, labels, w_full, grad_out):
    count = codes.shape[0]
    factor = 1.0 / math.sqrt(HD)
    values = dequantize(codes, scales)
    query = values[:, 0].reshape(count, HEADS, HD).astype(jnp.float32)
    keys = values[:, 1].reshape(count, HEADS, HD).astype(jnp.float32)
    value_rows = values[:, 2].reshape(count, HEADS, HD).astype(jnp.float32)
    scores = jnp.einsum('qhd,khd->hqk', query, keys) * factor
    same = labels[:, None] == labels[None, :]
    scores = jnp.where(same[None], scores, -jnp.inf)
    top = lax.optimization_barrier(jnp.max(scores, axis=-1, keepdims=True))
    weights = jnp.exp(scores - top)
    probs = weights / lax.optimization_barrier(jnp.sum(weights, axis=-1, keepdims=True))
    probs_b = probs.astype(jnp.bfloat16).astype(jnp.float32)
    context = jnp.einsum('hqk,khd->qhd', probs_b, value_rows).reshape(count, HW).astype(jnp.bfloat16)
    output = jnp.dot(context, w_full, preferred_element_type=jnp.float32).astype(jnp.bfloat16)
    grad_context = lax.dot_general(grad_out, w_full, (((1,), (1,)), ((), ())), preferred_element_type=jnp.float32)
    grad_context = grad_context.astype(jnp.bfloat16).reshape(count, HEADS, HD).astype(jnp.float32)
    grad_probs = jnp.einsum('qhd,khd->hqk', grad_context, value_rows)
    total = lax.optimization_barrier(jnp.sum(probs * grad_probs, axis=-1, keepdims=True))
    grad_scores = (probs * (grad_probs - total) * factor).astype(jnp.bfloat16).astype(jnp.float32)
    grad_query = jnp.einsum('hqk,khd->qhd', grad_scores, keys)
    grad_keys = jnp.einsum('hqk,qhd->khd', grad_scores, query)
    grad_values = jnp.einsum('hqk,qhd->khd', probs_b, grad_context)
    grads = jnp.stack([grad_query, grad_keys, grad_values], axis=1).reshape(count, 3, -1)
    blocks = scales.shape[-1]
    grads = (grads.reshape(count, 3, blocks, -1) * scales.astype(jnp.float32)[..., None]).reshape(count, 3, -1)
    term = lax.dot_general(context, grad_out, (((0,), (0,)), ((), ())), preferred_element_type=jnp.float32)
    return (output, grads.astype(jnp.bfloat16), term)

def pad_rows(array, fill):
    extra = jnp.full((array.shape[0], SLOT) + array.shape[2:], fill, array.dtype)
    return jnp.concatenate([array, extra], axis=1)

def corner(device, at_row, ndim):
    return (device.astype(jnp.int32), at_row.astype(jnp.int32)) + (jnp.int32(0),) * (ndim - 2)

def take_rows(buffer, device, at_row):
    return lax.dynamic_slice(buffer, corner(device, at_row, buffer.ndim), (1, SLOT) + buffer.shape[2:])

def place_rows(buffer, piece, device, at_row, length):
    old = take_rows(buffer, device, at_row)
    present = (jnp.arange(SLOT) < length).reshape((1, SLOT) + (1,) * (buffer.ndim - 2))
    return lax.dynamic_update_slice(buffer, jnp.where(present, piece, old), corner(device, at_row, buffer.ndim))

def balance_group(items):
    codes, scales, segments, kept, table = items
    inside = jnp.arange(ROWS)[None, :] < kept[:, None]
    start_codes = pad_rows(jnp.where(inside[:, :, None, None], codes, jnp.zeros_like(codes)), 0)
    start_scales = pad_rows(jnp.where(inside[:, :, None, None], scales, jnp.zeros_like(scales)), 0)
    start_labels = pad_rows(jnp.where(inside, segments, -1).astype(jnp.int32), -1)
    home_codes = pad_rows(codes, 0)
    home_scales = pad_rows(scales, 0)
    moved_by = jnp.array(offsets, jnp.int32)

    def step(index, state):
        bal_codes, bal_scales, labels = state
        index = index.astype(jnp.int32)
        source = index // 4
        route = index % 4
        entry = table[source, route]
        target = jnp.clip(source + moved_by[route], 0, N_DP - 1)
        bal_codes = place_rows(bal_codes, take_rows(home_codes, source, entry[0]), target, entry[2], entry[1])
        bal_scales = place_rows(bal_scales, take_rows(home_scales, source, entry[0]), target, entry[2], entry[1])
        marks = jnp.full((1, SLOT), 100000, jnp.int32) + route
        labels = place_rows(labels, marks, target, entry[2], entry[1])
        return (bal_codes, bal_scales, labels)
    bal_codes, bal_scales, labels = lax.fori_loop(0, N_DP * 4, step, (start_codes, start_scales, start_labels))
    return (bal_codes[:, :ROWS], bal_scales[:, :ROWS], labels[:, :ROWS])

def return_group(items):
    grads, kept, table = items
    inside = jnp.arange(ROWS)[None, :] < kept[:, None]
    home = pad_rows(jnp.where(inside[:, :, None, None], grads, jnp.zeros_like(grads)), 0)
    source_rows = pad_rows(grads, 0)
    moved_by = jnp.array(offsets, jnp.int32)

    def step(index, home):
        index = index.astype(jnp.int32)
        source = index // 4
        route = index % 4
        entry = table[source, route]
        target = jnp.clip(source + moved_by[route], 0, N_DP - 1)
        return place_rows(home, take_rows(source_rows, target, entry[2]), source, entry[0], entry[1])
    home = lax.fori_loop(0, N_DP * 4, step, home)
    return home[:, :ROWS]

def by_group(array):
    return jnp.swapaxes(array, 0, 1)

def reference(qkv_codes, block_scales, home_segments, kept_rows, pack_list, w_out, cotangent):
    bal_codes, bal_scales, labels = lax.map(balance_group, (by_group(qkv_codes), by_group(block_scales), by_group(home_segments), by_group(kept_rows), by_group(pack_list)))

    def per_device(total, item):
        codes, scales, marks, grad_out = item
        output, grads, term = local_layer(codes, scales, marks, w_out, grad_out)
        rounded = lax.optimization_barrier(term.astype(jnp.bfloat16))
        return (total + rounded.astype(jnp.float32), (output, grads))

    def per_data(item):
        total, (outputs, grads) = lax.scan(per_device, jnp.zeros((HW, D), jnp.float32), item)
        return (outputs, grads, total)
    outputs, grads, grad_w = lax.map(per_data, (by_group(bal_codes), by_group(bal_scales), by_group(labels), cotangent))
    home_grads = lax.map(return_group, (by_group(grads), by_group(kept_rows), by_group(pack_list)))
    return (outputs, by_group(home_grads), grad_w)
```

```python
import functools
import math

import jax
import jax.numpy as jnp
from jax import lax
from jax.experimental import pallas as pl
from jax.experimental.pallas import tpu as pltpu
from jax.sharding import PartitionSpec as P

HEADS = 8
OFFSETS = (1, -1, 2, -2)
SLOT = 16
LANES = 128
F32 = jnp.float32
BF16 = jnp.bfloat16
NT = (((1,), (1,)), ((), ()))
TN = (((0,), (0,)), ((), ()))


def shifted(block, axis, distance):
    devices = range(lax.axis_size(axis))
    route = [(i - distance, i) for i in devices if i - distance in devices]
    return lax.ppermute(block, axis, route)


def dot(a, b, dims=(((1,), (0,)), ((), ()))):
    return lax.dot_general(a, b, dims, preferred_element_type=F32)


def sent_spans(table, at):
    return [(table[0, d, at], table[1, d, at]) for d in range(4)]


def placed_spans(table, at, group):
    spans = []
    for d in range(4):
        source = at - OFFSETS[d]
        allowed = (source >= 0) & (source < group)
        source = jnp.clip(source, 0, group - 1)
        spans.append((table[2, d, source], jnp.where(allowed, table[1, d, source], 0)))
    return spans


def one_hot(spans, rows, slots_first):
    shape = (4 * SLOT, rows) if slots_first else (rows, 4 * SLOT)
    slot = lax.broadcasted_iota(jnp.int32, shape, 0 if slots_first else 1)
    row = lax.broadcasted_iota(jnp.int32, shape, 1 if slots_first else 0)
    hot = None
    for d, (first, length) in enumerate(spans):
        i = slot - SLOT * d
        here = (i >= 0) & (i < length) & (row == first + i)
        hot = here if hot is None else hot | here
    return jnp.where(hot, 1.0, 0.0).astype(BF16)


def expanded(select, scales):
    columns = dot(select, scales, NT)
    return jnp.concatenate(
        [
            jnp.broadcast_to(columns[:, b : b + 1], (select.shape[0], LANES))
            for b in range(scales.shape[0])
        ],
        axis=1,
    )


def window(head, size):
    low = head * size // LANES
    high = ((head + 1) * size - 1) // LANES + 1
    return low, high


def head_mask(head, size, rows):
    low, high = window(head, size)
    column = lax.broadcasted_iota(jnp.int32, (rows, (high - low) * LANES), 1) + low * LANES
    return (column >= head * size) & (column < (head + 1) * size)


def add_tiles(tiles, part, low):
    for i in range(part.shape[1] // LANES):
        piece = part[:, i * LANES : (i + 1) * LANES]
        tiles[low + i] = piece if tiles[low + i] is None else tiles[low + i] + piece


def pack_kernel(table, codes, scales, *sent):
    at = lax.axis_index("dp")
    rows = codes.shape[1]
    select = one_hot(sent_spans(table, at), rows, True)
    for c in range(3):
        values = dot(select, codes[c]) * expanded(select, scales[c])
        values = values.astype(BF16)
        for d in range(4):
            sent[d][c] = values[d * SLOT : (d + 1) * SLOT]


def forward_kernel(
    group, table, kept, segments, codes, scales, r0, r1, r2, r3, grad_out,
    term, context_out, balanced, probs_out, turned
):
    rows, width = codes.shape[1:]
    size = width // HEADS
    factor = 1.0 / math.sqrt(size)

    @pl.when(pl.program_id(0) == 0)
    def _():
        at = lax.axis_index("dp")
        keep = kept[0, 0]
        spans = placed_spans(table, at, group)
        place = one_hot(spans, rows, False)
        row = lax.broadcasted_iota(jnp.int32, (rows, rows), 0)
        lane = lax.broadcasted_iota(jnp.int32, (rows, rows), 1)
        eye = row == lane
        identity = jnp.where(eye, 1.0, 0.0).astype(BF16)
        along = jnp.broadcast_to(segments[...], (rows, rows))
        labels = jnp.where(lane < keep, along, -1)
        for d, (first, length) in enumerate(spans):
            labels = jnp.where((lane >= first) & (lane < first + length), 100000 + d, labels)
        labels = labels.astype(F32)
        down = jnp.sum(jnp.where(eye, labels, 0.0), axis=1, keepdims=True)
        same = labels == down
        column_row = lax.broadcasted_iota(jnp.int32, (rows, width), 0)
        for c in range(3):
            own = (codes[c].astype(F32) * expanded(identity, scales[c])).astype(BF16)
            own = jnp.where(column_row < keep, own.astype(F32), 0.0)
            arrived = jnp.concatenate([r0[c], r1[c], r2[c], r3[c]], axis=0)
            balanced[c] = (own + dot(place, arrived)).astype(BF16)
        tiles = [None] * (width // LANES)
        for head in range(HEADS):
            low, high = window(head, size)
            cut = slice(low * LANES, high * LANES)
            mask = head_mask(head, size, rows)
            query = balanced[0, :, cut]
            keys = jnp.where(mask, balanced[1, :, cut].astype(F32), 0.0).astype(BF16)
            values = jnp.where(mask, balanced[2, :, cut].astype(F32), 0.0).astype(BF16)
            scores = jnp.where(same, dot(query, keys, NT) * factor, -jnp.inf)
            weights = jnp.exp(scores - jnp.max(scores, axis=1, keepdims=True))
            probs = weights / jnp.sum(weights, axis=1, keepdims=True)
            probs_out[head] = probs
            add_tiles(tiles, dot(probs.astype(BF16), values), low)
        context = jnp.concatenate(tiles, axis=1)
        context_out[...] = context.astype(BF16)
        turned[...] = context.T.astype(BF16)

    term[...] = dot(turned[...], grad_out[...]).astype(BF16)


def backward_kernel(
    group, table, kept, w, grad_out, context, balanced, probs_in, scales,
    output, home, b0, b1, b2, b3, total_out, grad_context
):
    step = pl.program_id(0)
    rows, width = balanced.shape[1:]
    size = width // HEADS
    factor = 1.0 / math.sqrt(size)
    part = dot(context[...], w[...])

    @pl.when(step == 0)
    def _():
        total_out[...] = part

    @pl.when(step > 0)
    def _():
        total_out[...] += part

    grad_context[step] = dot(grad_out[...], w[...], NT).astype(BF16)

    @pl.when(step == pl.num_programs(0) - 1)
    def _():
        output[...] = total_out[...].astype(BF16)
        at = lax.axis_index("dp")
        keep = kept[0, 0]
        count = width // LANES
        grads = [[None] * count for _ in range(3)]
        for head in range(HEADS):
            low, high = window(head, size)
            cut = slice(low * LANES, high * LANES)
            mask = head_mask(head, size, rows)

            def masked(values):
                return jnp.where(mask, values.astype(F32), 0.0).astype(BF16)

            query = masked(balanced[0, :, cut])
            keys = masked(balanced[1, :, cut])
            values = balanced[2, :, cut]
            upstream = masked(jnp.concatenate([grad_context[i] for i in range(low, high)], axis=1))
            probs = probs_in[head]
            grad_probs = dot(upstream, values, NT)
            total = jnp.sum(probs * grad_probs, axis=1, keepdims=True)
            grad_scores = probs * (grad_probs - total) * factor
            add_tiles(grads[0], dot(grad_scores.astype(BF16), keys), low)
            add_tiles(grads[1], dot(grad_scores.T.astype(BF16), query), low)
            add_tiles(grads[2], dot(probs.T.astype(BF16), upstream), low)
        select = one_hot(placed_spans(table, at, group), rows, True)
        row = lax.broadcasted_iota(jnp.int32, (rows, rows), 0)
        lane = lax.broadcasted_iota(jnp.int32, (rows, rows), 1)
        identity = jnp.where((row == lane) & (row < keep), 1.0, 0.0).astype(BF16)
        for c in range(3):
            grad = jnp.concatenate(grads[c], axis=1)
            home[c] = (grad * expanded(identity, scales[c])).astype(BF16)
            back = dot(select, grad.astype(BF16)).astype(BF16)
            for d, ref in enumerate((b0, b1, b2, b3)):
                ref[c] = back[d * SLOT : (d + 1) * SLOT]


def return_kernel(table, home, scales, r0, r1, r2, r3, grad_codes):
    at = lax.axis_index("dp")
    rows = home.shape[1]
    place = one_hot(sent_spans(table, at), rows, False)
    row = lax.broadcasted_iota(jnp.int32, (rows, rows), 0)
    lane = lax.broadcasted_iota(jnp.int32, (rows, rows), 1)
    identity = jnp.where(row == lane, 1.0, 0.0).astype(BF16)
    for c in range(3):
        arrived = jnp.concatenate([r0[c], r1[c], r2[c], r3[c]], axis=0)
        moved = dot(place, arrived) * expanded(identity, scales[c])
        grad_codes[c] = (home[c].astype(F32) + moved).astype(BF16)


def whole(shape):
    return pl.BlockSpec(shape, lambda *_: (0,) * len(shape))


def local(qkv_codes, block_scales, home_segments, kept_rows, pack_list, w_out, cotangent):
    group = lax.axis_size("dp")
    codes = jnp.transpose(qkv_codes[0, 0], (1, 0, 2))
    scales = jnp.transpose(block_scales[0, 0], (1, 2, 0))
    segments = home_segments[0]
    table = jnp.transpose(pack_list[:, 0], (2, 1, 0))
    grad_out = cotangent[0, 0]
    _, rows, width = codes.shape
    depth = w_out.shape[1]
    blocks = scales.shape[1]
    smem = pl.BlockSpec(memory_space=pltpu.SMEM)
    params = pltpu.CompilerParams(vmem_limit_bytes=24 * 1024 * 1024)
    piece = jax.ShapeDtypeStruct((3, SLOT, width), BF16)
    piece_spec = whole((3, SLOT, width))
    codes_spec = whole((3, rows, width))
    scales_spec = whole((3, blocks, rows))

    w_full = lax.all_gather(w_out, "fsdp", axis=0, tiled=True)

    sent = pl.pallas_call(
        pack_kernel,
        out_shape=[piece] * 4,
        in_specs=[smem, codes_spec, scales_spec],
        out_specs=[piece_spec] * 4,
        compiler_params=params,
        name="pack",
    )(table, codes, scales)
    received = [shifted(sent[d], "dp", OFFSETS[d]) for d in range(4)]

    chunk = 256
    term, context, balanced, probs = pl.pallas_call(
        functools.partial(forward_kernel, group),
        grid=(depth // chunk,),
        out_shape=[
            jax.ShapeDtypeStruct((width, depth), BF16),
            jax.ShapeDtypeStruct((rows, width), BF16),
            jax.ShapeDtypeStruct((3, rows, width), BF16),
            jax.ShapeDtypeStruct((HEADS, rows, rows), F32),
        ],
        in_specs=[smem, smem, whole((1, rows)), codes_spec, scales_spec]
        + [piece_spec] * 4
        + [pl.BlockSpec((rows, chunk), lambda n: (0, n))],
        out_specs=[
            pl.BlockSpec((width, chunk), lambda n: (0, n)),
            whole((rows, width)),
            codes_spec,
            whole((HEADS, rows, rows)),
        ],
        scratch_shapes=[pltpu.VMEM((width, rows), BF16)],
        compiler_params=params,
        name="forward",
    )(table, kept_rows, segments, codes, scales, *received, grad_out)

    grad_w = lax.psum_scatter(term, "fsdp", scatter_dimension=0, tiled=True).astype(F32)

    output, home, *back = pl.pallas_call(
        functools.partial(backward_kernel, group),
        grid=(width // LANES,),
        out_shape=[
            jax.ShapeDtypeStruct((rows, depth), BF16),
            jax.ShapeDtypeStruct((3, rows, width), BF16),
        ]
        + [piece] * 4,
        in_specs=[
            smem,
            smem,
            pl.BlockSpec((LANES, depth), lambda n: (n, 0)),
            whole((rows, depth)),
            pl.BlockSpec((rows, LANES), lambda n: (0, n)),
            codes_spec,
            whole((HEADS, rows, rows)),
            scales_spec,
        ],
        out_specs=[whole((rows, depth)), codes_spec] + [piece_spec] * 4,
        scratch_shapes=[
            pltpu.VMEM((rows, depth), F32),
            pltpu.VMEM((width // LANES, rows, LANES), BF16),
        ],
        compiler_params=params,
        name="backward",
    )(table, kept_rows, w_full, grad_out, context, balanced, probs, scales)
    returned = [shifted(back[d], "dp", -OFFSETS[d]) for d in range(4)]

    grad_codes = pl.pallas_call(
        return_kernel,
        out_shape=jax.ShapeDtypeStruct((3, rows, width), BF16),
        in_specs=[smem, codes_spec, scales_spec] + [piece_spec] * 4,
        out_specs=codes_spec,
        compiler_params=params,
        name="restore",
    )(table, home, scales, *returned)
    grad_codes = jnp.transpose(grad_codes, (1, 0, 2))
    return (output[None, None], grad_codes[None, None], grad_w[None])


def solution(mesh):
    return jax.shard_map(
        local,
        mesh=mesh,
        in_specs=(
            P("dp", "fsdp", None, None, None),
            P("dp", "fsdp", None, None, None),
            P("dp", "fsdp", None),
            P("dp", "fsdp"),
            P(None, "fsdp", None, None),
            P("fsdp", None),
            P("dp", "fsdp", None, None),
        ),
        out_specs=(
            P("dp", "fsdp", None, None),
            P("dp", "fsdp", None, None, None),
            P("dp", "fsdp", None),
        ),
        check_vma=False,
    )
```

```python
import functools
import math

import jax
import jax.numpy as jnp
from jax import lax
from jax.experimental import pallas as pl
from jax.experimental.pallas import tpu as pltpu
from jax.sharding import PartitionSpec as P

HEADS = 8
OFFSETS = (1, -1, 2, -2)
SLOT = 16
LANES = 128
F32 = jnp.float32
BF16 = jnp.bfloat16
NT = (((1,), (1,)), ((), ()))
TN = (((0,), (0,)), ((), ()))


def shifted(block, axis, distance):
    devices = range(lax.axis_size(axis))
    route = [(i - distance, i) for i in devices if i - distance in devices]
    return lax.ppermute(block, axis, route)


def dot(a, b, dims=(((1,), (0,)), ((), ()))):
    return lax.dot_general(a, b, dims, preferred_element_type=F32)


def sent_spans(table, at):
    return [(table[0, d, at], table[1, d, at]) for d in range(4)]


def placed_spans(table, at, group):
    spans = []
    for d in range(4):
        source = at - OFFSETS[d]
        allowed = (source >= 0) & (source < group)
        source = jnp.clip(source, 0, group - 1)
        spans.append((table[2, d, source], jnp.where(allowed, table[1, d, source], 0)))
    return spans


def one_hot(spans, rows, slots_first):
    shape = (4 * SLOT, rows) if slots_first else (rows, 4 * SLOT)
    slot = lax.broadcasted_iota(jnp.int32, shape, 0 if slots_first else 1)
    row = lax.broadcasted_iota(jnp.int32, shape, 1 if slots_first else 0)
    hot = None
    for d, (first, length) in enumerate(spans):
        i = slot - SLOT * d
        here = (i >= 0) & (i < length) & (row == first + i)
        hot = here if hot is None else hot | here
    return jnp.where(hot, 1.0, 0.0).astype(BF16)


def expanded(select, scales):
    columns = dot(select, scales, NT)
    return jnp.concatenate(
        [
            jnp.broadcast_to(columns[:, b : b + 1], (select.shape[0], LANES))
            for b in range(scales.shape[0])
        ],
        axis=1,
    )


def window(head, size):
    low = head * size // LANES
    high = ((head + 1) * size - 1) // LANES + 1
    return low, high


def head_mask(head, size, rows):
    low, high = window(head, size)
    column = lax.broadcasted_iota(jnp.int32, (rows, (high - low) * LANES), 1) + low * LANES
    return (column >= head * size) & (column < (head + 1) * size)


def add_tiles(tiles, part, low):
    for i in range(part.shape[1] // LANES):
        piece = part[:, i * LANES : (i + 1) * LANES]
        tiles[low + i] = piece if tiles[low + i] is None else tiles[low + i] + piece


def pack_kernel(table, codes, scales, *sent):
    at = lax.axis_index("dp")
    rows = codes.shape[1]
    select = one_hot(sent_spans(table, at), rows, True)
    for c in range(3):
        values = dot(select, codes[c]) * expanded(select, scales[c])
        values = values.astype(BF16)
        for d in range(4):
            sent[d][c] = values[d * SLOT : (d + 1) * SLOT]


def split_order(width, half, core):
    count = width // 2
    part = width // HEADS // 2
    slot = lax.broadcasted_iota(jnp.int32, (1, count), 1)
    chip = jnp.zeros((1, count), jnp.int32)
    for x in range(1, HEADS):
        chip += jnp.where(slot >= x * part, 1, 0)
    side = core if half == 0 else 1 - core
    source = slot + part * chip + part * side
    row = lax.broadcasted_iota(jnp.int32, (width, count), 0)
    return jnp.where(row == source, 1.0, 0.0).astype(BF16)


def forward_kernel(
    group, table, kept, segments, codes, scales, r0, r1, r2, r3, grad_out,
    term_other, context_own, context_other, turned_own, orders, balanced, probs_out, turned
):
    rows, width = codes.shape[1:]
    size = width // HEADS
    factor = 1.0 / math.sqrt(size)

    @pl.when(pl.program_id(0) == 0)
    def _():
        at = lax.axis_index("dp")
        core = lax.rem(lax.axis_index("fsdp"), 2)
        keep = kept[0, 0]
        spans = placed_spans(table, at, group)
        place = one_hot(spans, rows, False)
        row = lax.broadcasted_iota(jnp.int32, (rows, rows), 0)
        lane = lax.broadcasted_iota(jnp.int32, (rows, rows), 1)
        eye = row == lane
        identity = jnp.where(eye, 1.0, 0.0).astype(BF16)
        along = jnp.broadcast_to(segments[...], (rows, rows))
        labels = jnp.where(lane < keep, along, -1)
        for d, (first, length) in enumerate(spans):
            labels = jnp.where((lane >= first) & (lane < first + length), 100000 + d, labels)
        labels = labels.astype(F32)
        down = jnp.sum(jnp.where(eye, labels, 0.0), axis=1, keepdims=True)
        same = labels == down
        column_row = lax.broadcasted_iota(jnp.int32, (rows, width), 0)
        for c in range(3):
            own = (codes[c].astype(F32) * expanded(identity, scales[c])).astype(BF16)
            own = jnp.where(column_row < keep, own.astype(F32), 0.0)
            arrived = jnp.concatenate([r0[c], r1[c], r2[c], r3[c]], axis=0)
            balanced[c] = (own + dot(place, arrived)).astype(BF16)
        tiles = [None] * (width // LANES)
        for head in range(HEADS):
            low, high = window(head, size)
            cut = slice(low * LANES, high * LANES)
            mask = head_mask(head, size, rows)
            query = balanced[0, :, cut]
            keys = jnp.where(mask, balanced[1, :, cut].astype(F32), 0.0).astype(BF16)
            values = jnp.where(mask, balanced[2, :, cut].astype(F32), 0.0).astype(BF16)
            scores = jnp.where(same, dot(query, keys, NT) * factor, -jnp.inf)
            weights = jnp.exp(scores - jnp.max(scores, axis=1, keepdims=True))
            probs = weights / jnp.sum(weights, axis=1, keepdims=True)
            probs_out[head] = probs
            add_tiles(tiles, dot(probs.astype(BF16), values), low)
        context = jnp.concatenate(tiles, axis=1).astype(BF16)
        for half, (side, flipped) in enumerate(((context_own, turned_own), (context_other, turned))):
            orders[half] = split_order(width, half, core)
            picked = dot(context, orders[half])
            side[...] = picked.astype(BF16)
            flipped[...] = picked.T.astype(BF16)

    term_other[...] = dot(turned[...], grad_out[...]).astype(BF16)


def fold_kernel(turned_own, grad_out, arrived, folded):
    own = dot(turned_own[...], grad_out[...]).astype(BF16)
    folded[...] = (own.astype(F32) + arrived[...].astype(F32)).astype(BF16)


def upstream_kernel(grad_out, w, grad_context):
    grad_context[...] = dot(grad_out[...], w[...], NT).astype(BF16)


def output_kernel(context_own, context_other, w_own, w_other, output):
    total = dot(context_own[...], w_own[...]) + dot(context_other[...], w_other[...])
    output[...] = total.astype(BF16)


def backward_kernel(
    group, table, kept, w_other, grad_out, upstream_own, orders, balanced, probs_in, scales,
    home, b0, b1, b2, b3, upstream_all
):
    rows, width = balanced.shape[1:]
    size = width // HEADS
    factor = 1.0 / math.sqrt(size)
    upstream_other = dot(grad_out[...], w_other[...], NT).astype(BF16)
    upstream_all[...] = (
        dot(upstream_own[...], orders[0], NT) + dot(upstream_other, orders[1], NT)
    ).astype(BF16)
    at = lax.axis_index("dp")
    keep = kept[0, 0]
    grads = [[None] * (width // LANES) for _ in range(3)]
    for head in range(HEADS):
        low, high = window(head, size)
        cut = slice(low * LANES, high * LANES)
        mask = head_mask(head, size, rows)

        def masked(values):
            return jnp.where(mask, values.astype(F32), 0.0).astype(BF16)

        query = masked(balanced[0, :, cut])
        keys = masked(balanced[1, :, cut])
        values = balanced[2, :, cut]
        upstream = masked(upstream_all[:, cut])
        probs = probs_in[head]
        grad_probs = dot(upstream, values, NT)
        total = jnp.sum(probs * grad_probs, axis=1, keepdims=True)
        grad_scores = probs * (grad_probs - total) * factor
        add_tiles(grads[0], dot(grad_scores.astype(BF16), keys), low)
        add_tiles(grads[1], dot(grad_scores.T.astype(BF16), query), low)
        add_tiles(grads[2], dot(probs.T.astype(BF16), upstream), low)
    select = one_hot(placed_spans(table, at, group), rows, True)
    row = lax.broadcasted_iota(jnp.int32, (rows, rows), 0)
    lane = lax.broadcasted_iota(jnp.int32, (rows, rows), 1)
    identity = jnp.where((row == lane) & (row < keep), 1.0, 0.0).astype(BF16)
    for c in range(3):
        grad = jnp.concatenate(grads[c], axis=1)
        home[c] = (grad * expanded(identity, scales[c])).astype(BF16)
        back = dot(select, grad.astype(BF16)).astype(BF16)
        for d, ref in enumerate((b0, b1, b2, b3)):
            ref[c] = back[d * SLOT : (d + 1) * SLOT]


def return_kernel(table, home, scales, r0, r1, r2, r3, grad_codes):
    at = lax.axis_index("dp")
    rows = home.shape[1]
    place = one_hot(sent_spans(table, at), rows, False)
    row = lax.broadcasted_iota(jnp.int32, (rows, rows), 0)
    lane = lax.broadcasted_iota(jnp.int32, (rows, rows), 1)
    identity = jnp.where(row == lane, 1.0, 0.0).astype(BF16)
    for c in range(3):
        arrived = jnp.concatenate([r0[c], r1[c], r2[c], r3[c]], axis=0)
        moved = dot(place, arrived) * expanded(identity, scales[c])
        grad_codes[c] = (home[c].astype(F32) + moved).astype(BF16)


def whole(shape):
    return pl.BlockSpec(shape, lambda *_: (0,) * len(shape))


def local(qkv_codes, block_scales, home_segments, kept_rows, pack_list, w_out, cotangent):
    group = lax.axis_size("dp")
    codes = jnp.transpose(qkv_codes[0, 0], (1, 0, 2))
    scales = jnp.transpose(block_scales[0, 0], (1, 2, 0))
    segments = home_segments[0]
    table = jnp.transpose(pack_list[:, 0], (2, 1, 0))
    grad_out = cotangent[0, 0]
    _, rows, width = codes.shape
    depth = w_out.shape[1]
    blocks = scales.shape[1]
    devices = lax.axis_size("fsdp")
    half = width // 2
    cores = [list(range(core, devices, 2)) for core in range(2)]
    swap = [(i, i + 1 - 2 * (i % 2)) for i in range(devices)]
    smem = pl.BlockSpec(memory_space=pltpu.SMEM)
    params = pltpu.CompilerParams(vmem_limit_bytes=48 * 1024 * 1024)
    small = pl.CostEstimate(flops=1, bytes_accessed=1, transcendentals=0)
    piece = jax.ShapeDtypeStruct((3, SLOT, width), BF16)
    piece_spec = whole((3, SLOT, width))
    codes_spec = whole((3, rows, width))
    scales_spec = whole((3, blocks, rows))

    w_own = lax.all_gather(w_out, "fsdp", axis=0, tiled=True, axis_index_groups=cores)

    sent = pl.pallas_call(
        pack_kernel,
        out_shape=[piece] * 4,
        in_specs=[smem, codes_spec, scales_spec],
        out_specs=[piece_spec] * 4,
        compiler_params=params,
        cost_estimate=small,
        name="pack",
    )(table, codes, scales)
    received = [shifted(sent[d], "dp", OFFSETS[d]) for d in range(4)]

    chunk = 256
    half_context = jax.ShapeDtypeStruct((rows, half), BF16)
    half_term = jax.ShapeDtypeStruct((half, depth), BF16)
    term_spec = pl.BlockSpec((half, chunk), lambda n: (0, n))
    grad_spec = pl.BlockSpec((rows, chunk), lambda n: (0, n))
    term_other, context_own, context_other, turned_own, orders, balanced, probs = pl.pallas_call(
        functools.partial(forward_kernel, group),
        grid=(depth // chunk,),
        out_shape=[
            half_term,
            half_context,
            half_context,
            jax.ShapeDtypeStruct((half, rows), BF16),
            jax.ShapeDtypeStruct((2, width, half), BF16),
            jax.ShapeDtypeStruct((3, rows, width), BF16),
            jax.ShapeDtypeStruct((HEADS, rows, rows), F32),
        ],
        in_specs=[smem, smem, whole((1, rows)), codes_spec, scales_spec]
        + [piece_spec] * 4
        + [grad_spec],
        out_specs=[
            term_spec,
            whole((rows, half)),
            whole((rows, half)),
            whole((half, rows)),
            whole((2, width, half)),
            codes_spec,
            whole((HEADS, rows, rows)),
        ],
        scratch_shapes=[pltpu.VMEM((half, rows), BF16)],
        compiler_params=params,
        cost_estimate=small,
        name="forward",
    )(table, kept_rows, segments, codes, scales, *received, grad_out)
    w_own, term_other = lax.optimization_barrier((w_own, term_other))
    arrived = lax.ppermute(term_other, "fsdp", swap)
    w_other = lax.ppermute(w_own, "fsdp", swap)
    folded = pl.pallas_call(
        fold_kernel,
        grid=(depth // chunk,),
        out_shape=half_term,
        in_specs=[whole((half, rows)), grad_spec, term_spec],
        out_specs=term_spec,
        compiler_params=params,
        name="fold",
    )(turned_own, grad_out, arrived)
    grad_w = lax.psum_scatter(
        folded, "fsdp", scatter_dimension=0, tiled=True, axis_index_groups=cores
    ).astype(F32)

    upstream_own = pl.pallas_call(
        upstream_kernel,
        out_shape=half_context,
        compiler_params=params,
        name="upstream",
    )(grad_out, w_own)
    home, *back = pl.pallas_call(
        functools.partial(backward_kernel, group),
        out_shape=[jax.ShapeDtypeStruct((3, rows, width), BF16)] + [piece] * 4,
        in_specs=[
            smem,
            smem,
            whole((half, depth)),
            whole((rows, depth)),
            whole((rows, half)),
            whole((2, width, half)),
            codes_spec,
            whole((HEADS, rows, rows)),
            scales_spec,
        ],
        out_specs=[codes_spec] + [piece_spec] * 4,
        scratch_shapes=[pltpu.VMEM((rows, width), BF16)],
        compiler_params=params,
        name="backward",
    )(table, kept_rows, w_other, grad_out, upstream_own, orders, balanced, probs, scales)
    weight_spec = pl.BlockSpec((half, chunk), lambda n: (0, n))
    output = pl.pallas_call(
        output_kernel,
        grid=(depth // chunk,),
        out_shape=jax.ShapeDtypeStruct((rows, depth), BF16),
        in_specs=[whole((rows, half))] * 2 + [weight_spec] * 2,
        out_specs=grad_spec,
        compiler_params=params,
        name="project",
    )(context_own, context_other, w_own, w_other)
    returned = [shifted(back[d], "dp", -OFFSETS[d]) for d in range(4)]

    grad_codes = pl.pallas_call(
        return_kernel,
        out_shape=jax.ShapeDtypeStruct((3, rows, width), BF16),
        in_specs=[smem, codes_spec, scales_spec] + [piece_spec] * 4,
        out_specs=codes_spec,
        compiler_params=params,
        name="restore",
    )(table, home, scales, *returned)
    grad_codes = jnp.transpose(grad_codes, (1, 0, 2))
    return (output[None, None], grad_codes[None, None], grad_w[None])


def solution(mesh):
    return jax.shard_map(
        local,
        mesh=mesh,
        in_specs=(
            P("dp", "fsdp", None, None, None),
            P("dp", "fsdp", None, None, None),
            P("dp", "fsdp", None),
            P("dp", "fsdp"),
            P(None, "fsdp", None, None),
            P("fsdp", None),
            P("dp", "fsdp", None, None),
        ),
        out_specs=(
            P("dp", "fsdp", None, None),
            P("dp", "fsdp", None, None, None),
            P("dp", "fsdp", None),
        ),
        check_vma=False,
    )
```

```python
import functools
import math

import jax
import jax.numpy as jnp
from jax import lax
from jax.experimental import pallas as pl
from jax.experimental.pallas import tpu as pltpu
from jax.sharding import PartitionSpec as P

HEADS = 8
OFFSETS = (1, -1, 2, -2)
SLOT = 16
LANES = 128
F32 = jnp.float32
BF16 = jnp.bfloat16
NT = (((1,), (1,)), ((), ()))
TN = (((0,), (0,)), ((), ()))


def shifted(block, axis, distance):
    devices = range(lax.axis_size(axis))
    route = [(i - distance, i) for i in devices if i - distance in devices]
    return lax.ppermute(block, axis, route)


def dot(a, b, dims=(((1,), (0,)), ((), ()))):
    return lax.dot_general(a, b, dims, preferred_element_type=F32)


def sent_spans(table, at):
    return [(table[0, d, at], table[1, d, at]) for d in range(4)]


def placed_spans(table, at, group):
    spans = []
    for d in range(4):
        source = at - OFFSETS[d]
        allowed = (source >= 0) & (source < group)
        source = jnp.clip(source, 0, group - 1)
        spans.append((table[2, d, source], jnp.where(allowed, table[1, d, source], 0)))
    return spans


def one_hot(spans, rows, slots_first):
    shape = (4 * SLOT, rows) if slots_first else (rows, 4 * SLOT)
    slot = lax.broadcasted_iota(jnp.int32, shape, 0 if slots_first else 1)
    row = lax.broadcasted_iota(jnp.int32, shape, 1 if slots_first else 0)
    hot = None
    for d, (first, length) in enumerate(spans):
        i = slot - SLOT * d
        here = (i >= 0) & (i < length) & (row == first + i)
        hot = here if hot is None else hot | here
    return jnp.where(hot, 1.0, 0.0).astype(BF16)


def expanded(select, scales):
    columns = dot(select, scales, NT)
    return jnp.concatenate(
        [
            jnp.broadcast_to(columns[:, b : b + 1], (select.shape[0], LANES))
            for b in range(scales.shape[0])
        ],
        axis=1,
    )


def window(head, size):
    low = head * size // LANES
    high = ((head + 1) * size - 1) // LANES + 1
    return low, high


def head_mask(head, size, rows):
    low, high = window(head, size)
    column = lax.broadcasted_iota(jnp.int32, (rows, (high - low) * LANES), 1) + low * LANES
    return (column >= head * size) & (column < (head + 1) * size)


def add_tiles(tiles, part, low):
    for i in range(part.shape[1] // LANES):
        piece = part[:, i * LANES : (i + 1) * LANES]
        tiles[low + i] = piece if tiles[low + i] is None else tiles[low + i] + piece


def pack_kernel(table, codes, scales, *sent):
    at = lax.axis_index("dp")
    rows = codes.shape[1]
    select = one_hot(sent_spans(table, at), rows, True)
    for c in range(3):
        values = dot(select, codes[c]) * expanded(select, scales[c])
        values = values.astype(BF16)
        for d in range(4):
            sent[d][c] = values[d * SLOT : (d + 1) * SLOT]


def split_order(width, half, core):
    count = width // 2
    part = width // HEADS // 2
    slot = lax.broadcasted_iota(jnp.int32, (1, count), 1)
    chip = jnp.zeros((1, count), jnp.int32)
    for x in range(1, HEADS):
        chip += jnp.where(slot >= x * part, 1, 0)
    side = core if half == 0 else 1 - core
    source = slot + part * chip + part * side
    row = lax.broadcasted_iota(jnp.int32, (width, count), 0)
    return jnp.where(row == source, 1.0, 0.0).astype(BF16)


def forward_kernel(
    group, table, kept, segments, codes, scales, r0, r1, r2, r3, grad_out,
    term_other, context_out, turned_own, balanced, probs_out, turned
):
    rows, width = codes.shape[1:]
    size = width // HEADS
    factor = 1.0 / math.sqrt(size)

    @pl.when(pl.program_id(0) == 0)
    def _():
        at = lax.axis_index("dp")
        core = lax.rem(lax.axis_index("fsdp"), 2)
        keep = kept[0, 0]
        spans = placed_spans(table, at, group)
        place = one_hot(spans, rows, False)
        row = lax.broadcasted_iota(jnp.int32, (rows, rows), 0)
        lane = lax.broadcasted_iota(jnp.int32, (rows, rows), 1)
        eye = row == lane
        identity = jnp.where(eye, 1.0, 0.0).astype(BF16)
        along = jnp.broadcast_to(segments[...], (rows, rows))
        labels = jnp.where(lane < keep, along, -1)
        for d, (first, length) in enumerate(spans):
            labels = jnp.where((lane >= first) & (lane < first + length), 100000 + d, labels)
        labels = labels.astype(F32)
        down = jnp.sum(jnp.where(eye, labels, 0.0), axis=1, keepdims=True)
        same = labels == down
        column_row = lax.broadcasted_iota(jnp.int32, (rows, width), 0)
        for c in range(3):
            own = (codes[c].astype(F32) * expanded(identity, scales[c])).astype(BF16)
            own = jnp.where(column_row < keep, own.astype(F32), 0.0)
            arrived = jnp.concatenate([r0[c], r1[c], r2[c], r3[c]], axis=0)
            balanced[c] = (own + dot(place, arrived)).astype(BF16)
        tiles = [None] * (width // LANES)
        for head in range(HEADS):
            low, high = window(head, size)
            cut = slice(low * LANES, high * LANES)
            mask = head_mask(head, size, rows)
            query = balanced[0, :, cut]
            keys = jnp.where(mask, balanced[1, :, cut].astype(F32), 0.0).astype(BF16)
            values = jnp.where(mask, balanced[2, :, cut].astype(F32), 0.0).astype(BF16)
            scores = jnp.where(same, dot(query, keys, NT) * factor, -jnp.inf)
            weights = jnp.exp(scores - jnp.max(scores, axis=1, keepdims=True))
            probs = weights / jnp.sum(weights, axis=1, keepdims=True)
            probs_out[head] = probs
            add_tiles(tiles, dot(probs.astype(BF16), values), low)
        context = jnp.concatenate(tiles, axis=1).astype(BF16)
        context_out[...] = context
        part = width // HEADS // 2
        for half, flipped in enumerate((turned_own, turned)):
            across = dot(context, split_order(width, half, core)).T
            upper, lower = [
                [across[x * part + low : x * part + low + part // 2] for x in range(HEADS)]
                for low in (0, part // 2)
            ]
            flipped[0] = jnp.concatenate(upper + lower, axis=0).astype(BF16)
            flipped[1] = across.astype(BF16)

    term_other[...] = dot(turned[pl.program_id(0)], grad_out[...]).astype(BF16)


def fold_kernel(turned_own, grad_out, arrived, paired, plain):
    own = dot(turned_own[0], grad_out[...]).astype(BF16)
    folded = (own.astype(F32) + arrived[...].astype(F32)).astype(BF16)

    @pl.when(pl.program_id(0) == 0)
    def _():
        count = folded.shape[0] // 2
        paired[...] = jnp.concatenate([folded[:count], folded[count:]], axis=1)

    @pl.when(pl.program_id(0) == 1)
    def _():
        plain[...] = folded


def join_kernel(paired, plain, grad_w):
    columns = plain.shape[1]
    left = paired[...].astype(F32)
    left = jnp.concatenate([left[:, :columns], left[:, columns:]], axis=0)
    grad_w[...] = jnp.concatenate([left, plain[...].astype(F32)], axis=1)


def output_kernel(context, w, output):
    output[...] = dot(context[...], w[...]).astype(BF16)


def backward_kernel(
    group, table, kept, w, grad_out, balanced, probs_in, scales,
    home, b0, b1, b2, b3, upstream_all
):
    step = pl.program_id(0)
    rows, width = balanced.shape[1:]
    size = width // HEADS
    factor = 1.0 / math.sqrt(size)
    upstream_all[step] = dot(grad_out[...], w[...], NT).astype(BF16)

    @pl.when(step == pl.num_programs(0) - 1)
    def _():
        at = lax.axis_index("dp")
        keep = kept[0, 0]
        grads = [[None] * (width // LANES) for _ in range(3)]
        for head in range(HEADS):
            low, high = window(head, size)
            cut = slice(low * LANES, high * LANES)
            mask = head_mask(head, size, rows)

            def masked(values):
                return jnp.where(mask, values.astype(F32), 0.0).astype(BF16)

            query = masked(balanced[0, :, cut])
            keys = masked(balanced[1, :, cut])
            values = balanced[2, :, cut]
            upstream = masked(jnp.concatenate([upstream_all[i] for i in range(low, high)], axis=1))
            probs = probs_in[head]
            grad_probs = dot(upstream, values, NT)
            total = jnp.sum(probs * grad_probs, axis=1, keepdims=True)
            grad_scores = probs * (grad_probs - total) * factor
            add_tiles(grads[0], dot(grad_scores.astype(BF16), keys), low)
            add_tiles(grads[1], dot(grad_scores.T.astype(BF16), query), low)
            add_tiles(grads[2], dot(probs.T.astype(BF16), upstream), low)
        select = one_hot(placed_spans(table, at, group), rows, True)
        row = lax.broadcasted_iota(jnp.int32, (rows, rows), 0)
        lane = lax.broadcasted_iota(jnp.int32, (rows, rows), 1)
        identity = jnp.where((row == lane) & (row < keep), 1.0, 0.0).astype(BF16)
        for c in range(3):
            grad = jnp.concatenate(grads[c], axis=1)
            home[c] = (grad * expanded(identity, scales[c])).astype(BF16)
            back = dot(select, grad.astype(BF16)).astype(BF16)
            for d, ref in enumerate((b0, b1, b2, b3)):
                ref[c] = back[d * SLOT : (d + 1) * SLOT]


def return_kernel(table, home, scales, r0, r1, r2, r3, grad_codes):
    at = lax.axis_index("dp")
    rows = home.shape[1]
    place = one_hot(sent_spans(table, at), rows, False)
    row = lax.broadcasted_iota(jnp.int32, (rows, rows), 0)
    lane = lax.broadcasted_iota(jnp.int32, (rows, rows), 1)
    identity = jnp.where(row == lane, 1.0, 0.0).astype(BF16)
    for c in range(3):
        arrived = jnp.concatenate([r0[c], r1[c], r2[c], r3[c]], axis=0)
        moved = dot(place, arrived) * expanded(identity, scales[c])
        grad_codes[c] = (home[c].astype(F32) + moved).astype(BF16)


def whole(shape):
    return pl.BlockSpec(shape, lambda *_: (0,) * len(shape))


def local(qkv_codes, block_scales, home_segments, kept_rows, pack_list, w_out, cotangent):
    group = lax.axis_size("dp")
    codes = jnp.transpose(qkv_codes[0, 0], (1, 0, 2))
    scales = jnp.transpose(block_scales[0, 0], (1, 2, 0))
    segments = home_segments[0]
    table = jnp.transpose(pack_list[:, 0], (2, 1, 0))
    grad_out = cotangent[0, 0]
    _, rows, width = codes.shape
    depth = w_out.shape[1]
    blocks = scales.shape[1]
    devices = lax.axis_size("fsdp")
    half = width // 2
    cores = [list(range(core, devices, 2)) for core in range(2)]
    swap = [(i, i + 1 - 2 * (i % 2)) for i in range(devices)]
    smem = pl.BlockSpec(memory_space=pltpu.SMEM)
    params = pltpu.CompilerParams(vmem_limit_bytes=56 * 1024 * 1024)
    light = pltpu.CompilerParams(vmem_limit_bytes=24 * 1024 * 1024)
    small = pl.CostEstimate(flops=1, bytes_accessed=1, transcendentals=0)
    piece = jax.ShapeDtypeStruct((3, SLOT, width), BF16)
    piece_spec = whole((3, SLOT, width))
    codes_spec = whole((3, rows, width))
    scales_spec = whole((3, blocks, rows))

    w_full = lax.all_gather(w_out, "fsdp", axis=0, tiled=True)

    sent = pl.pallas_call(
        pack_kernel,
        out_shape=[piece] * 4,
        in_specs=[smem, codes_spec, scales_spec],
        out_specs=[piece_spec] * 4,
        compiler_params=params,
        cost_estimate=small,
        name="pack",
    )(table, codes, scales)
    received = [shifted(sent[d], "dp", OFFSETS[d]) for d in range(4)]

    span = depth // 2
    term_spec = pl.BlockSpec((half, span), lambda n: (0, n))
    grad_spec = pl.BlockSpec((rows, span), lambda n: (0, n))
    term_other, context, turned_own, balanced, probs = pl.pallas_call(
        functools.partial(forward_kernel, group),
        grid=(2,),
        out_shape=[
            jax.ShapeDtypeStruct((half, depth), BF16),
            jax.ShapeDtypeStruct((rows, width), BF16),
            jax.ShapeDtypeStruct((2, half, rows), BF16),
            jax.ShapeDtypeStruct((3, rows, width), BF16),
            jax.ShapeDtypeStruct((HEADS, rows, rows), F32),
        ],
        in_specs=[smem, smem, whole((1, rows)), codes_spec, scales_spec]
        + [piece_spec] * 4
        + [grad_spec],
        out_specs=[
            term_spec,
            whole((rows, width)),
            whole((2, half, rows)),
            codes_spec,
            whole((HEADS, rows, rows)),
        ],
        scratch_shapes=[pltpu.VMEM((2, half, rows), BF16)],
        compiler_params=params,
        cost_estimate=small,
        name="forward",
    )(table, kept_rows, segments, codes, scales, *received, grad_out)
    arrived = lax.ppermute(term_other, "fsdp", swap)
    paired, plain = pl.pallas_call(
        fold_kernel,
        grid=(2,),
        out_shape=[
            jax.ShapeDtypeStruct((half // 2, depth), BF16),
            jax.ShapeDtypeStruct((half, span), BF16),
        ],
        in_specs=[
            pl.BlockSpec((1, half, rows), lambda n: (n, 0, 0)),
            grad_spec,
            term_spec,
        ],
        out_specs=[whole((half // 2, depth)), whole((half, span))],
        compiler_params=light,
        name="fold",
    )(turned_own, grad_out, arrived)
    plain = lax.psum_scatter(
        plain, "fsdp", scatter_dimension=0, tiled=True, axis_index_groups=cores
    )
    paired = lax.psum_scatter(
        paired, "fsdp", scatter_dimension=0, tiled=True, axis_index_groups=cores
    )
    balanced, paired = lax.optimization_barrier((balanced, paired))

    home, *back = pl.pallas_call(
        functools.partial(backward_kernel, group),
        grid=(width // LANES,),
        out_shape=[jax.ShapeDtypeStruct((3, rows, width), BF16)] + [piece] * 4,
        in_specs=[
            smem,
            smem,
            pl.BlockSpec((LANES, depth), lambda n: (n, 0)),
            whole((rows, depth)),
            codes_spec,
            whole((HEADS, rows, rows)),
            scales_spec,
        ],
        out_specs=[codes_spec] + [piece_spec] * 4,
        scratch_shapes=[pltpu.VMEM((width // LANES, rows, LANES), BF16)],
        compiler_params=params,
        name="backward",
    )(table, kept_rows, w_full, grad_out, balanced, probs, scales)
    chunk = 256
    output = pl.pallas_call(
        output_kernel,
        grid=(depth // chunk,),
        out_shape=jax.ShapeDtypeStruct((rows, depth), BF16),
        in_specs=[whole((rows, width)), pl.BlockSpec((width, chunk), lambda n: (0, n))],
        out_specs=pl.BlockSpec((rows, chunk), lambda n: (0, n)),
        compiler_params=params,
        name="project",
    )(context, w_full)
    returned = [shifted(back[d], "dp", -OFFSETS[d]) for d in range(4)]

    grad_codes = pl.pallas_call(
        return_kernel,
        out_shape=jax.ShapeDtypeStruct((3, rows, width), BF16),
        in_specs=[smem, codes_spec, scales_spec] + [piece_spec] * 4,
        out_specs=codes_spec,
        compiler_params=light,
        name="restore",
    )(table, home, scales, *returned)
    paired, grad_codes = lax.optimization_barrier((paired, grad_codes))
    grad_w = pl.pallas_call(
        join_kernel,
        out_shape=jax.ShapeDtypeStruct(w_out.shape, F32),
        compiler_params=light,
        name="join",
    )(paired, plain)
    grad_codes = jnp.transpose(grad_codes, (1, 0, 2))
    return (output[None, None], grad_codes[None, None], grad_w[None])


def solution(mesh):
    return jax.shard_map(
        local,
        mesh=mesh,
        in_specs=(
            P("dp", "fsdp", None, None, None),
            P("dp", "fsdp", None, None, None),
            P("dp", "fsdp", None),
            P("dp", "fsdp"),
            P(None, "fsdp", None, None),
            P("fsdp", None),
            P("dp", "fsdp", None, None),
        ),
        out_specs=(
            P("dp", "fsdp", None, None),
            P("dp", "fsdp", None, None, None),
            P("dp", "fsdp", None),
        ),
        check_vma=False,
    )
```

```python
import functools
import math

import jax
import jax.numpy as jnp
from jax import lax
from jax.experimental import pallas as pl
from jax.experimental.pallas import tpu as pltpu
from jax.sharding import PartitionSpec as P

HEADS = 8
OFFSETS = (1, -1, 2, -2)
SLOT = 16
LANES = 128
F32 = jnp.float32
BF16 = jnp.bfloat16
NT = (((1,), (1,)), ((), ()))
TN = (((0,), (0,)), ((), ()))


def shifted(block, axis, distance):
    devices = range(lax.axis_size(axis))
    route = [(i - distance, i) for i in devices if i - distance in devices]
    return lax.ppermute(block, axis, route)


def dot(a, b, dims=(((1,), (0,)), ((), ()))):
    return lax.dot_general(a, b, dims, preferred_element_type=F32)


def sent_spans(table, at):
    return [(table[0, d, at], table[1, d, at]) for d in range(4)]


def placed_spans(table, at, group):
    spans = []
    for d in range(4):
        source = at - OFFSETS[d]
        allowed = (source >= 0) & (source < group)
        source = jnp.clip(source, 0, group - 1)
        spans.append((table[2, d, source], jnp.where(allowed, table[1, d, source], 0)))
    return spans


def one_hot(spans, rows, slots_first):
    shape = (4 * SLOT, rows) if slots_first else (rows, 4 * SLOT)
    slot = lax.broadcasted_iota(jnp.int32, shape, 0 if slots_first else 1)
    row = lax.broadcasted_iota(jnp.int32, shape, 1 if slots_first else 0)
    hot = None
    for d, (first, length) in enumerate(spans):
        i = slot - SLOT * d
        here = (i >= 0) & (i < length) & (row == first + i)
        hot = here if hot is None else hot | here
    return jnp.where(hot, 1.0, 0.0).astype(BF16)


def expanded(select, scales):
    columns = dot(select, scales, NT)
    return jnp.concatenate(
        [
            jnp.broadcast_to(columns[:, b : b + 1], (select.shape[0], LANES))
            for b in range(scales.shape[0])
        ],
        axis=1,
    )


def window(head, size):
    low = head * size // LANES
    high = ((head + 1) * size - 1) // LANES + 1
    return low, high


def head_mask(head, size, rows):
    low, high = window(head, size)
    column = lax.broadcasted_iota(jnp.int32, (rows, (high - low) * LANES), 1) + low * LANES
    return (column >= head * size) & (column < (head + 1) * size)


def add_tiles(tiles, part, low):
    for i in range(part.shape[1] // LANES):
        piece = part[:, i * LANES : (i + 1) * LANES]
        tiles[low + i] = piece if tiles[low + i] is None else tiles[low + i] + piece


def pack_kernel(table, codes, scales, *sent):
    at = lax.axis_index("dp")
    rows = codes.shape[1]
    select = one_hot(sent_spans(table, at), rows, True)
    for c in range(3):
        values = dot(select, codes[c]) * expanded(select, scales[c])
        values = values.astype(BF16)
        for d in range(4):
            sent[d][c] = values[d * SLOT : (d + 1) * SLOT]


def split_order(width, half, core):
    count = width // 2
    part = width // HEADS // 2
    slot = lax.broadcasted_iota(jnp.int32, (1, count), 1)
    chip = jnp.zeros((1, count), jnp.int32)
    for x in range(1, HEADS):
        chip += jnp.where(slot >= x * part, 1, 0)
    side = core if half == 0 else 1 - core
    source = slot + part * chip + part * side
    row = lax.broadcasted_iota(jnp.int32, (width, count), 0)
    return jnp.where(row == source, 1.0, 0.0).astype(BF16)


def forward_kernel(
    group, table, kept, segments, codes, scales, r0, r1, r2, r3, grad_out,
    term_other, context_out, turned_own, balanced, probs_out, turned
):
    rows, width = codes.shape[1:]
    size = width // HEADS
    factor = 1.0 / math.sqrt(size)

    @pl.when(pl.program_id(0) == 0)
    def _():
        at = lax.axis_index("dp")
        core = lax.rem(lax.axis_index("fsdp"), 2)
        keep = kept[0, 0]
        spans = placed_spans(table, at, group)
        place = one_hot(spans, rows, False)
        row = lax.broadcasted_iota(jnp.int32, (rows, rows), 0)
        lane = lax.broadcasted_iota(jnp.int32, (rows, rows), 1)
        eye = row == lane
        identity = jnp.where(eye, 1.0, 0.0).astype(BF16)
        along = jnp.broadcast_to(segments[...], (rows, rows))
        labels = jnp.where(lane < keep, along, -1)
        for d, (first, length) in enumerate(spans):
            labels = jnp.where((lane >= first) & (lane < first + length), 100000 + d, labels)
        labels = labels.astype(F32)
        down = jnp.sum(jnp.where(eye, labels, 0.0), axis=1, keepdims=True)
        same = labels == down
        column_row = lax.broadcasted_iota(jnp.int32, (rows, width), 0)
        for c in range(3):
            own = (codes[c].astype(F32) * expanded(identity, scales[c])).astype(BF16)
            own = jnp.where(column_row < keep, own.astype(F32), 0.0)
            arrived = jnp.concatenate([r0[c], r1[c], r2[c], r3[c]], axis=0)
            balanced[c] = (own + dot(place, arrived)).astype(BF16)
        tiles = [None] * (width // LANES)
        for head in range(HEADS):
            low, high = window(head, size)
            cut = slice(low * LANES, high * LANES)
            mask = head_mask(head, size, rows)
            query = balanced[0, :, cut]
            keys = jnp.where(mask, balanced[1, :, cut].astype(F32), 0.0).astype(BF16)
            values = jnp.where(mask, balanced[2, :, cut].astype(F32), 0.0).astype(BF16)
            scores = jnp.where(same, dot(query, keys, NT) * factor, -jnp.inf)
            weights = jnp.exp(scores - jnp.max(scores, axis=1, keepdims=True))
            probs = weights / jnp.sum(weights, axis=1, keepdims=True)
            probs_out[head] = probs
            add_tiles(tiles, dot(probs.astype(BF16), values), low)
        context = jnp.concatenate(tiles, axis=1).astype(BF16)
        context_out[...] = context
        for half, flipped in enumerate((turned_own, turned)):
            flipped[...] = dot(context, split_order(width, half, core)).T.astype(BF16)

    term_other[...] = dot(turned[...], grad_out[...]).astype(BF16)


def fold_kernel(turned_own, grad_out, arrived, folded):
    own = dot(turned_own[...], grad_out[...]).astype(BF16)
    folded[...] = (own.astype(F32) + arrived[...].astype(F32)).astype(BF16)


def widen_kernel(narrow, wide):
    wide[...] = narrow[...].astype(F32)


def output_kernel(context, w, output):
    output[...] = dot(context[...], w[...]).astype(BF16)


def backward_kernel(
    group, table, kept, w, grad_out, balanced, probs_in, scales,
    home, b0, b1, b2, b3, upstream_all
):
    rows, width = balanced.shape[1:]
    size = width // HEADS
    factor = 1.0 / math.sqrt(size)
    upstream_all[...] = dot(grad_out[...], w[...], NT).astype(BF16)
    at = lax.axis_index("dp")
    keep = kept[0, 0]
    grads = [[None] * (width // LANES) for _ in range(3)]
    for head in range(HEADS):
        low, high = window(head, size)
        cut = slice(low * LANES, high * LANES)
        mask = head_mask(head, size, rows)

        def masked(values):
            return jnp.where(mask, values.astype(F32), 0.0).astype(BF16)

        query = masked(balanced[0, :, cut])
        keys = masked(balanced[1, :, cut])
        values = balanced[2, :, cut]
        upstream = masked(upstream_all[:, cut])
        probs = probs_in[head]
        grad_probs = dot(upstream, values, NT)
        total = jnp.sum(probs * grad_probs, axis=1, keepdims=True)
        grad_scores = probs * (grad_probs - total) * factor
        add_tiles(grads[0], dot(grad_scores.astype(BF16), keys), low)
        add_tiles(grads[1], dot(grad_scores.T.astype(BF16), query), low)
        add_tiles(grads[2], dot(probs.T.astype(BF16), upstream), low)
    select = one_hot(placed_spans(table, at, group), rows, True)
    row = lax.broadcasted_iota(jnp.int32, (rows, rows), 0)
    lane = lax.broadcasted_iota(jnp.int32, (rows, rows), 1)
    identity = jnp.where((row == lane) & (row < keep), 1.0, 0.0).astype(BF16)
    for c in range(3):
        grad = jnp.concatenate(grads[c], axis=1)
        home[c] = (grad * expanded(identity, scales[c])).astype(BF16)
        back = dot(select, grad.astype(BF16)).astype(BF16)
        for d, ref in enumerate((b0, b1, b2, b3)):
            ref[c] = back[d * SLOT : (d + 1) * SLOT]


def return_kernel(table, home, scales, r0, r1, r2, r3, grad_codes):
    at = lax.axis_index("dp")
    rows = home.shape[1]
    place = one_hot(sent_spans(table, at), rows, False)
    row = lax.broadcasted_iota(jnp.int32, (rows, rows), 0)
    lane = lax.broadcasted_iota(jnp.int32, (rows, rows), 1)
    identity = jnp.where(row == lane, 1.0, 0.0).astype(BF16)
    for c in range(3):
        arrived = jnp.concatenate([r0[c], r1[c], r2[c], r3[c]], axis=0)
        moved = dot(place, arrived) * expanded(identity, scales[c])
        grad_codes[c] = (home[c].astype(F32) + moved).astype(BF16)


def whole(shape):
    return pl.BlockSpec(shape, lambda *_: (0,) * len(shape))


def local(qkv_codes, block_scales, home_segments, kept_rows, pack_list, w_out, cotangent):
    group = lax.axis_size("dp")
    codes = jnp.transpose(qkv_codes[0, 0], (1, 0, 2))
    scales = jnp.transpose(block_scales[0, 0], (1, 2, 0))
    segments = home_segments[0]
    table = jnp.transpose(pack_list[:, 0], (2, 1, 0))
    grad_out = cotangent[0, 0]
    _, rows, width = codes.shape
    depth = w_out.shape[1]
    blocks = scales.shape[1]
    devices = lax.axis_size("fsdp")
    half = width // 2
    cores = [list(range(core, devices, 2)) for core in range(2)]
    swap = [(i, i + 1 - 2 * (i % 2)) for i in range(devices)]
    smem = pl.BlockSpec(memory_space=pltpu.SMEM)
    params = pltpu.CompilerParams(vmem_limit_bytes=56 * 1024 * 1024)
    light = pltpu.CompilerParams(vmem_limit_bytes=24 * 1024 * 1024)
    small = pl.CostEstimate(flops=1, bytes_accessed=1, transcendentals=0)
    piece = jax.ShapeDtypeStruct((3, SLOT, width), BF16)
    piece_spec = whole((3, SLOT, width))
    codes_spec = whole((3, rows, width))
    scales_spec = whole((3, blocks, rows))

    w_full = lax.all_gather(w_out, "fsdp", axis=0, tiled=True)

    sent = pl.pallas_call(
        pack_kernel,
        out_shape=[piece] * 4,
        in_specs=[smem, codes_spec, scales_spec],
        out_specs=[piece_spec] * 4,
        compiler_params=params,
        cost_estimate=small,
        name="pack",
    )(table, codes, scales)
    received = [shifted(sent[d], "dp", OFFSETS[d]) for d in range(4)]

    span = depth // 2
    term_spec = pl.BlockSpec((half, span), lambda n: (0, n))
    grad_spec = pl.BlockSpec((rows, span), lambda n: (0, n))
    term_other, context, turned_own, balanced, probs = pl.pallas_call(
        functools.partial(forward_kernel, group),
        grid=(2,),
        out_shape=[
            jax.ShapeDtypeStruct((half, depth), BF16),
            jax.ShapeDtypeStruct((rows, width), BF16),
            jax.ShapeDtypeStruct((half, rows), BF16),
            jax.ShapeDtypeStruct((3, rows, width), BF16),
            jax.ShapeDtypeStruct((HEADS, rows, rows), F32),
        ],
        in_specs=[smem, smem, whole((1, rows)), codes_spec, scales_spec]
        + [piece_spec] * 4
        + [grad_spec],
        out_specs=[
            term_spec,
            whole((rows, width)),
            whole((half, rows)),
            codes_spec,
            whole((HEADS, rows, rows)),
        ],
        scratch_shapes=[pltpu.VMEM((half, rows), BF16)],
        compiler_params=params,
        cost_estimate=small,
        name="forward",
    )(table, kept_rows, segments, codes, scales, *received, grad_out)
    arrived = lax.ppermute(term_other, "fsdp", swap)
    folded = pl.pallas_call(
        fold_kernel,
        grid=(2,),
        out_shape=jax.ShapeDtypeStruct((half, depth), BF16),
        in_specs=[whole((half, rows)), grad_spec, term_spec],
        out_specs=term_spec,
        compiler_params=light,
        name="fold",
    )(turned_own, grad_out, arrived)
    balanced, folded = lax.optimization_barrier((balanced, folded))
    scattered = lax.psum_scatter(
        folded, "fsdp", scatter_dimension=0, tiled=True, axis_index_groups=cores
    )

    home, *back = pl.pallas_call(
        functools.partial(backward_kernel, group),
        out_shape=[jax.ShapeDtypeStruct((3, rows, width), BF16)] + [piece] * 4,
        in_specs=[
            smem,
            smem,
            whole((width, depth)),
            whole((rows, depth)),
            codes_spec,
            whole((HEADS, rows, rows)),
            scales_spec,
        ],
        out_specs=[codes_spec] + [piece_spec] * 4,
        scratch_shapes=[pltpu.VMEM((rows, width), BF16)],
        compiler_params=light,
        name="backward",
    )(table, kept_rows, w_full, grad_out, balanced, probs, scales)
    chunk = 256
    output = pl.pallas_call(
        output_kernel,
        grid=(depth // chunk,),
        out_shape=jax.ShapeDtypeStruct((rows, depth), BF16),
        in_specs=[whole((rows, width)), pl.BlockSpec((width, chunk), lambda n: (0, n))],
        out_specs=pl.BlockSpec((rows, chunk), lambda n: (0, n)),
        compiler_params=light,
        name="project",
    )(context, w_full)
    returned = [shifted(back[d], "dp", -OFFSETS[d]) for d in range(4)]

    grad_codes = pl.pallas_call(
        return_kernel,
        out_shape=jax.ShapeDtypeStruct((3, rows, width), BF16),
        in_specs=[smem, codes_spec, scales_spec] + [piece_spec] * 4,
        out_specs=codes_spec,
        compiler_params=light,
        name="restore",
    )(table, home, scales, *returned)
    grad_w = pl.pallas_call(
        widen_kernel,
        out_shape=jax.ShapeDtypeStruct(w_out.shape, F32),
        compiler_params=params,
        name="widen",
    )(scattered)
    grad_codes = jnp.transpose(grad_codes, (1, 0, 2))
    return (output[None, None], grad_codes[None, None], grad_w[None])


def solution(mesh):
    return jax.shard_map(
        local,
        mesh=mesh,
        in_specs=(
            P("dp", "fsdp", None, None, None),
            P("dp", "fsdp", None, None, None),
            P("dp", "fsdp", None),
            P("dp", "fsdp"),
            P(None, "fsdp", None, None),
            P("fsdp", None),
            P("dp", "fsdp", None, None),
        ),
        out_specs=(
            P("dp", "fsdp", None, None),
            P("dp", "fsdp", None, None, None),
            P("dp", "fsdp", None),
        ),
        check_vma=False,
    )
```

```python
import functools
import math

import jax
import jax.numpy as jnp
from jax import lax
from jax.experimental import pallas as pl
from jax.experimental.pallas import tpu as pltpu
from jax.sharding import PartitionSpec as P

HEADS = 8
OFFSETS = (1, -1, 2, -2)
SLOT = 16
LANES = 128
F32 = jnp.float32
BF16 = jnp.bfloat16
NT = (((1,), (1,)), ((), ()))
TN = (((0,), (0,)), ((), ()))


def shifted(block, axis, distance):
    devices = range(lax.axis_size(axis))
    route = [(i - distance, i) for i in devices if i - distance in devices]
    return lax.ppermute(block, axis, route)


def dot(a, b, dims=(((1,), (0,)), ((), ()))):
    return lax.dot_general(a, b, dims, preferred_element_type=F32)


def sent_spans(table, at):
    return [(table[0, d, at], table[1, d, at]) for d in range(4)]


def placed_spans(table, at, group):
    spans = []
    for d in range(4):
        source = at - OFFSETS[d]
        allowed = (source >= 0) & (source < group)
        source = jnp.clip(source, 0, group - 1)
        spans.append((table[2, d, source], jnp.where(allowed, table[1, d, source], 0)))
    return spans


def one_hot(spans, rows, slots_first):
    shape = (4 * SLOT, rows) if slots_first else (rows, 4 * SLOT)
    slot = lax.broadcasted_iota(jnp.int32, shape, 0 if slots_first else 1)
    row = lax.broadcasted_iota(jnp.int32, shape, 1 if slots_first else 0)
    hot = None
    for d, (first, length) in enumerate(spans):
        i = slot - SLOT * d
        here = (i >= 0) & (i < length) & (row == first + i)
        hot = here if hot is None else hot | here
    return jnp.where(hot, 1.0, 0.0).astype(BF16)


def expanded(select, scales):
    columns = dot(select, scales, NT)
    return jnp.concatenate(
        [
            jnp.broadcast_to(columns[:, b : b + 1], (select.shape[0], LANES))
            for b in range(scales.shape[0])
        ],
        axis=1,
    )


def window(head, size):
    low = head * size // LANES
    high = ((head + 1) * size - 1) // LANES + 1
    return low, high


def head_mask(head, size, rows):
    low, high = window(head, size)
    column = lax.broadcasted_iota(jnp.int32, (rows, (high - low) * LANES), 1) + low * LANES
    return (column >= head * size) & (column < (head + 1) * size)


def add_tiles(tiles, part, low):
    for i in range(part.shape[1] // LANES):
        piece = part[:, i * LANES : (i + 1) * LANES]
        tiles[low + i] = piece if tiles[low + i] is None else tiles[low + i] + piece


def pack_kernel(table, codes, scales, *sent):
    at = lax.axis_index("dp")
    rows = codes.shape[1]
    select = one_hot(sent_spans(table, at), rows, True)
    for c in range(3):
        values = dot(select, codes[c]) * expanded(select, scales[c])
        values = values.astype(BF16)
        for d in range(4):
            sent[d][c] = values[d * SLOT : (d + 1) * SLOT]


def split_order(width, half, core):
    count = width // 2
    part = width // HEADS // 2
    slot = lax.broadcasted_iota(jnp.int32, (1, count), 1)
    chip = jnp.zeros((1, count), jnp.int32)
    for x in range(1, HEADS):
        chip += jnp.where(slot >= x * part, 1, 0)
    side = core if half == 0 else 1 - core
    source = slot + part * chip + part * side
    row = lax.broadcasted_iota(jnp.int32, (width, count), 0)
    return jnp.where(row == source, 1.0, 0.0).astype(BF16)


def forward_kernel(
    group, table, kept, segments, codes, scales, r0, r1, r2, r3, grad_out,
    term_other, context_out, turned_own, balanced, probs_out, turned
):
    rows, width = codes.shape[1:]
    size = width // HEADS
    factor = 1.0 / math.sqrt(size)

    @pl.when(pl.program_id(0) == 0)
    def _():
        at = lax.axis_index("dp")
        core = lax.rem(lax.axis_index("fsdp"), 2)
        keep = kept[0, 0]
        spans = placed_spans(table, at, group)
        place = one_hot(spans, rows, False)
        row = lax.broadcasted_iota(jnp.int32, (rows, rows), 0)
        lane = lax.broadcasted_iota(jnp.int32, (rows, rows), 1)
        eye = row == lane
        identity = jnp.where(eye, 1.0, 0.0).astype(BF16)
        along = jnp.broadcast_to(segments[...], (rows, rows))
        labels = jnp.where(lane < keep, along, -1)
        for d, (first, length) in enumerate(spans):
            labels = jnp.where((lane >= first) & (lane < first + length), 100000 + d, labels)
        labels = labels.astype(F32)
        down = jnp.sum(jnp.where(eye, labels, 0.0), axis=1, keepdims=True)
        same = labels == down
        column_row = lax.broadcasted_iota(jnp.int32, (rows, width), 0)
        for c in range(3):
            own = (codes[c].astype(F32) * expanded(identity, scales[c])).astype(BF16)
            own = jnp.where(column_row < keep, own.astype(F32), 0.0)
            arrived = jnp.concatenate([r0[c], r1[c], r2[c], r3[c]], axis=0)
            balanced[c] = (own + dot(place, arrived)).astype(BF16)
        tiles = [None] * (width // LANES)
        for head in range(HEADS):
            low, high = window(head, size)
            cut = slice(low * LANES, high * LANES)
            mask = head_mask(head, size, rows)
            query = balanced[0, :, cut]
            keys = jnp.where(mask, balanced[1, :, cut].astype(F32), 0.0).astype(BF16)
            values = jnp.where(mask, balanced[2, :, cut].astype(F32), 0.0).astype(BF16)
            scores = jnp.where(same, dot(query, keys, NT) * factor, -jnp.inf)
            weights = jnp.exp(scores - jnp.max(scores, axis=1, keepdims=True))
            probs = weights / jnp.sum(weights, axis=1, keepdims=True)
            probs_out[head] = probs
            add_tiles(tiles, dot(probs.astype(BF16), values), low)
        context = jnp.concatenate(tiles, axis=1).astype(BF16)
        context_out[...] = context
        for half, flipped in enumerate((turned_own, turned)):
            flipped[...] = dot(context, split_order(width, half, core)).T.astype(BF16)

    term_other[...] = dot(turned[...], grad_out[...]).astype(BF16)


def fold_kernel(turned_own, grad_out, arrived, folded):
    own = dot(turned_own[...], grad_out[...]).astype(BF16)
    folded[...] = (own.astype(F32) + arrived[...].astype(F32)).astype(BF16)


def widen_kernel(_, narrow, wide):
    wide[...] = narrow[...].astype(F32)


def output_kernel(context, w, output):
    output[...] = dot(context[...], w[...]).astype(BF16)


def backward_kernel(
    group, table, kept, w, grad_out, balanced, probs_in, scales,
    home, b0, b1, b2, b3, upstream_all
):
    rows, width = balanced.shape[1:]
    size = width // HEADS
    factor = 1.0 / math.sqrt(size)
    upstream_all[...] = dot(grad_out[...], w[...], NT).astype(BF16)
    at = lax.axis_index("dp")
    keep = kept[0, 0]
    grads = [[None] * (width // LANES) for _ in range(3)]
    for head in range(HEADS):
        low, high = window(head, size)
        cut = slice(low * LANES, high * LANES)
        mask = head_mask(head, size, rows)

        def masked(values):
            return jnp.where(mask, values.astype(F32), 0.0).astype(BF16)

        query = masked(balanced[0, :, cut])
        keys = masked(balanced[1, :, cut])
        values = balanced[2, :, cut]
        upstream = masked(upstream_all[:, cut])
        probs = probs_in[head]
        grad_probs = dot(upstream, values, NT)
        total = jnp.sum(probs * grad_probs, axis=1, keepdims=True)
        grad_scores = probs * (grad_probs - total) * factor
        add_tiles(grads[0], dot(grad_scores.astype(BF16), keys), low)
        add_tiles(grads[1], dot(grad_scores.T.astype(BF16), query), low)
        add_tiles(grads[2], dot(probs.T.astype(BF16), upstream), low)
    select = one_hot(placed_spans(table, at, group), rows, True)
    row = lax.broadcasted_iota(jnp.int32, (rows, rows), 0)
    lane = lax.broadcasted_iota(jnp.int32, (rows, rows), 1)
    identity = jnp.where((row == lane) & (row < keep), 1.0, 0.0).astype(BF16)
    for c in range(3):
        grad = jnp.concatenate(grads[c], axis=1)
        home[c] = (grad * expanded(identity, scales[c])).astype(BF16)
        back = dot(select, grad.astype(BF16)).astype(BF16)
        for d, ref in enumerate((b0, b1, b2, b3)):
            ref[c] = back[d * SLOT : (d + 1) * SLOT]


def return_kernel(table, home, scales, r0, r1, r2, r3, grad_codes):
    at = lax.axis_index("dp")
    rows = home.shape[1]
    place = one_hot(sent_spans(table, at), rows, False)
    row = lax.broadcasted_iota(jnp.int32, (rows, rows), 0)
    lane = lax.broadcasted_iota(jnp.int32, (rows, rows), 1)
    identity = jnp.where(row == lane, 1.0, 0.0).astype(BF16)
    for c in range(3):
        arrived = jnp.concatenate([r0[c], r1[c], r2[c], r3[c]], axis=0)
        moved = dot(place, arrived) * expanded(identity, scales[c])
        grad_codes[c] = (home[c].astype(F32) + moved).astype(BF16)


def whole(shape):
    return pl.BlockSpec(shape, lambda *_: (0,) * len(shape))


def local(qkv_codes, block_scales, home_segments, kept_rows, pack_list, w_out, cotangent):
    group = lax.axis_size("dp")
    codes = jnp.transpose(qkv_codes[0, 0], (1, 0, 2))
    scales = jnp.transpose(block_scales[0, 0], (1, 2, 0))
    segments = home_segments[0]
    table = jnp.transpose(pack_list[:, 0], (2, 1, 0))
    grad_out = cotangent[0, 0]
    _, rows, width = codes.shape
    depth = w_out.shape[1]
    blocks = scales.shape[1]
    devices = lax.axis_size("fsdp")
    half = width // 2
    cores = [list(range(core, devices, 2)) for core in range(2)]
    swap = [(i, i + 1 - 2 * (i % 2)) for i in range(devices)]
    smem = pl.BlockSpec(memory_space=pltpu.SMEM)
    params = pltpu.CompilerParams(vmem_limit_bytes=56 * 1024 * 1024)
    light = pltpu.CompilerParams(vmem_limit_bytes=24 * 1024 * 1024)
    small = pl.CostEstimate(flops=1, bytes_accessed=1, transcendentals=0)
    piece = jax.ShapeDtypeStruct((3, SLOT, width), BF16)
    piece_spec = whole((3, SLOT, width))
    codes_spec = whole((3, rows, width))
    scales_spec = whole((3, blocks, rows))

    w_full = lax.all_gather(w_out, "fsdp", axis=0, tiled=True)

    sent = pl.pallas_call(
        pack_kernel,
        out_shape=[piece] * 4,
        in_specs=[smem, codes_spec, scales_spec],
        out_specs=[piece_spec] * 4,
        compiler_params=params,
        cost_estimate=small,
        name="pack",
    )(table, codes, scales)
    received = [shifted(sent[d], "dp", OFFSETS[d]) for d in range(4)]

    span = depth // 2
    term_spec = pl.BlockSpec((half, span), lambda n: (0, n))
    grad_spec = pl.BlockSpec((rows, span), lambda n: (0, n))
    term_other, context, turned_own, balanced, probs = pl.pallas_call(
        functools.partial(forward_kernel, group),
        grid=(2,),
        out_shape=[
            jax.ShapeDtypeStruct((half, depth), BF16),
            jax.ShapeDtypeStruct((rows, width), BF16),
            jax.ShapeDtypeStruct((half, rows), BF16),
            jax.ShapeDtypeStruct((3, rows, width), BF16),
            jax.ShapeDtypeStruct((HEADS, rows, rows), F32),
        ],
        in_specs=[smem, smem, whole((1, rows)), codes_spec, scales_spec]
        + [piece_spec] * 4
        + [grad_spec],
        out_specs=[
            term_spec,
            whole((rows, width)),
            whole((half, rows)),
            codes_spec,
            whole((HEADS, rows, rows)),
        ],
        scratch_shapes=[pltpu.VMEM((half, rows), BF16)],
        compiler_params=params,
        cost_estimate=small,
        name="forward",
    )(table, kept_rows, segments, codes, scales, *received, grad_out)
    arrived = lax.ppermute(term_other, "fsdp", swap)
    folded = pl.pallas_call(
        fold_kernel,
        grid=(2,),
        out_shape=jax.ShapeDtypeStruct((half, depth), BF16),
        in_specs=[whole((half, rows)), grad_spec, term_spec],
        out_specs=term_spec,
        compiler_params=light,
        name="fold",
    )(turned_own, grad_out, arrived)
    balanced, folded = lax.optimization_barrier((balanced, folded))
    scattered = lax.psum_scatter(
        folded, "fsdp", scatter_dimension=0, tiled=True, axis_index_groups=cores
    )

    home, *back = pl.pallas_call(
        functools.partial(backward_kernel, group),
        out_shape=[jax.ShapeDtypeStruct((3, rows, width), BF16)] + [piece] * 4,
        in_specs=[
            smem,
            smem,
            whole((width, depth)),
            whole((rows, depth)),
            codes_spec,
            whole((HEADS, rows, rows)),
            scales_spec,
        ],
        out_specs=[codes_spec] + [piece_spec] * 4,
        scratch_shapes=[pltpu.VMEM((rows, width), BF16)],
        compiler_params=params,
        name="backward",
    )(table, kept_rows, w_full, grad_out, balanced, probs, scales)
    chunk = 256
    output = pl.pallas_call(
        output_kernel,
        grid=(depth // chunk,),
        out_shape=jax.ShapeDtypeStruct((rows, depth), BF16),
        in_specs=[whole((rows, width)), pl.BlockSpec((width, chunk), lambda n: (0, n))],
        out_specs=pl.BlockSpec((rows, chunk), lambda n: (0, n)),
        compiler_params=params,
        name="project",
    )(context, w_full)
    returned = [shifted(back[d], "dp", -OFFSETS[d]) for d in range(4)]

    grad_codes = pl.pallas_call(
        return_kernel,
        out_shape=jax.ShapeDtypeStruct((3, rows, width), BF16),
        in_specs=[smem, codes_spec, scales_spec] + [piece_spec] * 4,
        out_specs=codes_spec,
        compiler_params=light,
        name="restore",
    )(table, home, scales, *returned)
    gate, grad_codes, output = lax.optimization_barrier((kept_rows, grad_codes, output))
    grad_w = pl.pallas_call(
        widen_kernel,
        out_shape=jax.ShapeDtypeStruct(w_out.shape, F32),
        in_specs=[smem, whole(w_out.shape)],
        out_specs=whole(w_out.shape),
        compiler_params=params,
        name="widen",
    )(gate, scattered)
    grad_codes = jnp.transpose(grad_codes, (1, 0, 2))
    return (output[None, None], grad_codes[None, None], grad_w[None])


def solution(mesh):
    return jax.shard_map(
        local,
        mesh=mesh,
        in_specs=(
            P("dp", "fsdp", None, None, None),
            P("dp", "fsdp", None, None, None),
            P("dp", "fsdp", None),
            P("dp", "fsdp"),
            P(None, "fsdp", None, None),
            P("fsdp", None),
            P("dp", "fsdp", None, None),
        ),
        out_specs=(
            P("dp", "fsdp", None, None),
            P("dp", "fsdp", None, None, None),
            P("dp", "fsdp", None),
        ),
        check_vma=False,
    )
```

```python
import functools
import math

import jax
import jax.numpy as jnp
from jax import lax
from jax.experimental import pallas as pl
from jax.experimental.pallas import tpu as pltpu
from jax.sharding import PartitionSpec as P

HEADS = 8
OFFSETS = (1, -1, 2, -2)
SLOT = 16
LANES = 128
F32 = jnp.float32
BF16 = jnp.bfloat16
NT = (((1,), (1,)), ((), ()))
TN = (((0,), (0,)), ((), ()))


def shifted(block, axis, distance):
    devices = range(lax.axis_size(axis))
    route = [(i - distance, i) for i in devices if i - distance in devices]
    return lax.ppermute(block, axis, route)


def dot(a, b, dims=(((1,), (0,)), ((), ()))):
    return lax.dot_general(a, b, dims, preferred_element_type=F32)


def sent_spans(table, at):
    return [(table[0, d, at], table[1, d, at]) for d in range(4)]


def placed_spans(table, at, group):
    spans = []
    for d in range(4):
        source = at - OFFSETS[d]
        allowed = (source >= 0) & (source < group)
        source = jnp.clip(source, 0, group - 1)
        spans.append((table[2, d, source], jnp.where(allowed, table[1, d, source], 0)))
    return spans


def one_hot(spans, rows, slots_first):
    shape = (4 * SLOT, rows) if slots_first else (rows, 4 * SLOT)
    slot = lax.broadcasted_iota(jnp.int32, shape, 0 if slots_first else 1)
    row = lax.broadcasted_iota(jnp.int32, shape, 1 if slots_first else 0)
    hot = None
    for d, (first, length) in enumerate(spans):
        i = slot - SLOT * d
        here = (i >= 0) & (i < length) & (row == first + i)
        hot = here if hot is None else hot | here
    return jnp.where(hot, 1.0, 0.0).astype(BF16)


def expanded(select, scales):
    columns = dot(select, scales, NT)
    return jnp.concatenate(
        [
            jnp.broadcast_to(columns[:, b : b + 1], (select.shape[0], LANES))
            for b in range(scales.shape[0])
        ],
        axis=1,
    )


def window(head, size):
    low = head * size // LANES
    high = ((head + 1) * size - 1) // LANES + 1
    return low, high


def head_mask(head, size, rows):
    low, high = window(head, size)
    column = lax.broadcasted_iota(jnp.int32, (rows, (high - low) * LANES), 1) + low * LANES
    return (column >= head * size) & (column < (head + 1) * size)


def add_tiles(tiles, part, low):
    for i in range(part.shape[1] // LANES):
        piece = part[:, i * LANES : (i + 1) * LANES]
        tiles[low + i] = piece if tiles[low + i] is None else tiles[low + i] + piece


def pack_kernel(table, codes, scales, *sent):
    at = lax.axis_index("dp")
    rows = codes.shape[1]
    select = one_hot(sent_spans(table, at), rows, True)
    for c in range(3):
        values = dot(select, codes[c]) * expanded(select, scales[c])
        values = values.astype(BF16)
        for d in range(4):
            sent[d][c] = values[d * SLOT : (d + 1) * SLOT]


def split_order(width, half, core):
    count = width // 2
    part = width // HEADS // 2
    slot = lax.broadcasted_iota(jnp.int32, (1, count), 1)
    chip = jnp.zeros((1, count), jnp.int32)
    for x in range(1, HEADS):
        chip += jnp.where(slot >= x * part, 1, 0)
    side = core if half == 0 else 1 - core
    source = slot + part * chip + part * side
    row = lax.broadcasted_iota(jnp.int32, (width, count), 0)
    return jnp.where(row == source, 1.0, 0.0).astype(BF16)


def forward_kernel(
    group, table, kept, segments, codes, scales, r0, r1, r2, r3, grad_out,
    term_other, context_out, turned_own, balanced, probs_out, turned
):
    rows, width = codes.shape[1:]
    size = width // HEADS
    factor = 1.0 / math.sqrt(size)

    @pl.when(pl.program_id(0) == 0)
    def _():
        at = lax.axis_index("dp")
        core = lax.rem(lax.axis_index("fsdp"), 2)
        keep = kept[0, 0]
        spans = placed_spans(table, at, group)
        place = one_hot(spans, rows, False)
        row = lax.broadcasted_iota(jnp.int32, (rows, rows), 0)
        lane = lax.broadcasted_iota(jnp.int32, (rows, rows), 1)
        eye = row == lane
        identity = jnp.where(eye, 1.0, 0.0).astype(BF16)
        along = jnp.broadcast_to(segments[...], (rows, rows))
        labels = jnp.where(lane < keep, along, -1)
        for d, (first, length) in enumerate(spans):
            labels = jnp.where((lane >= first) & (lane < first + length), 100000 + d, labels)
        labels = labels.astype(F32)
        down = jnp.sum(jnp.where(eye, labels, 0.0), axis=1, keepdims=True)
        same = labels == down
        column_row = lax.broadcasted_iota(jnp.int32, (rows, width), 0)
        for c in range(3):
            own = (codes[c].astype(F32) * expanded(identity, scales[c])).astype(BF16)
            own = jnp.where(column_row < keep, own.astype(F32), 0.0)
            arrived = jnp.concatenate([r0[c], r1[c], r2[c], r3[c]], axis=0)
            balanced[c] = (own + dot(place, arrived)).astype(BF16)
        tiles = [None] * (width // LANES)
        for head in range(HEADS):
            low, high = window(head, size)
            cut = slice(low * LANES, high * LANES)
            mask = head_mask(head, size, rows)
            query = balanced[0, :, cut]
            keys = jnp.where(mask, balanced[1, :, cut].astype(F32), 0.0).astype(BF16)
            values = jnp.where(mask, balanced[2, :, cut].astype(F32), 0.0).astype(BF16)
            scores = jnp.where(same, dot(query, keys, NT) * factor, -jnp.inf)
            weights = jnp.exp(scores - jnp.max(scores, axis=1, keepdims=True))
            probs = weights / jnp.sum(weights, axis=1, keepdims=True)
            probs_out[head] = probs
            add_tiles(tiles, dot(probs.astype(BF16), values), low)
        context = jnp.concatenate(tiles, axis=1).astype(BF16)
        context_out[...] = context
        for half, flipped in enumerate((turned_own, turned)):
            flipped[...] = dot(context, split_order(width, half, core)).T.astype(BF16)

    term_other[...] = dot(turned[...], grad_out[...]).astype(BF16)


def fold_kernel(turned_own, grad_out, arrived, folded):
    own = dot(turned_own[...], grad_out[...]).astype(BF16)
    folded[...] = (own.astype(F32) + arrived[...].astype(F32)).astype(BF16)


def widen_kernel(_, narrow, wide):
    wide[...] = narrow[...].astype(F32)


def output_kernel(context, w, output):
    output[...] = dot(context[...], w[...]).astype(BF16)


def backward_kernel(
    group, table, kept, w, grad_out, balanced, probs_in, scales,
    home, b0, b1, b2, b3, upstream_all
):
    rows, width = balanced.shape[1:]
    size = width // HEADS
    factor = 1.0 / math.sqrt(size)
    upstream_all[...] = dot(grad_out[...], w[...], NT).astype(BF16)
    at = lax.axis_index("dp")
    keep = kept[0, 0]
    grads = [[None] * (width // LANES) for _ in range(3)]
    for head in range(HEADS):
        low, high = window(head, size)
        cut = slice(low * LANES, high * LANES)
        mask = head_mask(head, size, rows)

        def masked(values):
            return jnp.where(mask, values.astype(F32), 0.0).astype(BF16)

        query = masked(balanced[0, :, cut])
        keys = masked(balanced[1, :, cut])
        values = balanced[2, :, cut]
        upstream = masked(upstream_all[:, cut])
        probs = probs_in[head]
        grad_probs = dot(upstream, values, NT)
        total = jnp.sum(probs * grad_probs, axis=1, keepdims=True)
        grad_scores = probs * (grad_probs - total) * factor
        add_tiles(grads[0], dot(grad_scores.astype(BF16), keys), low)
        add_tiles(grads[1], dot(grad_scores.T.astype(BF16), query), low)
        add_tiles(grads[2], dot(probs.T.astype(BF16), upstream), low)
    select = one_hot(placed_spans(table, at, group), rows, True)
    row = lax.broadcasted_iota(jnp.int32, (rows, rows), 0)
    lane = lax.broadcasted_iota(jnp.int32, (rows, rows), 1)
    identity = jnp.where((row == lane) & (row < keep), 1.0, 0.0).astype(BF16)
    for c in range(3):
        grad = jnp.concatenate(grads[c], axis=1)
        home[c] = (grad * expanded(identity, scales[c])).astype(BF16)
        back = dot(select, grad.astype(BF16)).astype(BF16)
        for d, ref in enumerate((b0, b1, b2, b3)):
            ref[c] = back[d * SLOT : (d + 1) * SLOT]


def return_kernel(table, home, scales, r0, r1, r2, r3, _, grad_codes):
    at = lax.axis_index("dp")
    rows = home.shape[1]
    place = one_hot(sent_spans(table, at), rows, False)
    row = lax.broadcasted_iota(jnp.int32, (rows, rows), 0)
    lane = lax.broadcasted_iota(jnp.int32, (rows, rows), 1)
    identity = jnp.where(row == lane, 1.0, 0.0).astype(BF16)
    for c in range(3):
        arrived = jnp.concatenate([r0[c], r1[c], r2[c], r3[c]], axis=0)
        moved = dot(place, arrived) * expanded(identity, scales[c])
        grad_codes[c] = (home[c].astype(F32) + moved).astype(BF16)


def whole(shape):
    return pl.BlockSpec(shape, lambda *_: (0,) * len(shape))


def local(qkv_codes, block_scales, home_segments, kept_rows, pack_list, w_out, cotangent):
    group = lax.axis_size("dp")
    codes = jnp.transpose(qkv_codes[0, 0], (1, 0, 2))
    scales = jnp.transpose(block_scales[0, 0], (1, 2, 0))
    segments = home_segments[0]
    table = jnp.transpose(pack_list[:, 0], (2, 1, 0))
    grad_out = cotangent[0, 0]
    _, rows, width = codes.shape
    depth = w_out.shape[1]
    blocks = scales.shape[1]
    devices = lax.axis_size("fsdp")
    half = width // 2
    cores = [list(range(core, devices, 2)) for core in range(2)]
    swap = [(i, i + 1 - 2 * (i % 2)) for i in range(devices)]
    smem = pl.BlockSpec(memory_space=pltpu.SMEM)
    params = pltpu.CompilerParams(vmem_limit_bytes=56 * 1024 * 1024)
    light = pltpu.CompilerParams(vmem_limit_bytes=24 * 1024 * 1024)
    small = pl.CostEstimate(flops=1, bytes_accessed=1, transcendentals=0)
    piece = jax.ShapeDtypeStruct((3, SLOT, width), BF16)
    piece_spec = whole((3, SLOT, width))
    codes_spec = whole((3, rows, width))
    scales_spec = whole((3, blocks, rows))

    w_full = lax.all_gather(w_out, "fsdp", axis=0, tiled=True)

    sent = pl.pallas_call(
        pack_kernel,
        out_shape=[piece] * 4,
        in_specs=[smem, codes_spec, scales_spec],
        out_specs=[piece_spec] * 4,
        compiler_params=params,
        cost_estimate=small,
        name="pack",
    )(table, codes, scales)
    received = [shifted(sent[d], "dp", OFFSETS[d]) for d in range(4)]

    span = depth // 2
    term_spec = pl.BlockSpec((half, span), lambda n: (0, n))
    grad_spec = pl.BlockSpec((rows, span), lambda n: (0, n))
    term_other, context, turned_own, balanced, probs = pl.pallas_call(
        functools.partial(forward_kernel, group),
        grid=(2,),
        out_shape=[
            jax.ShapeDtypeStruct((half, depth), BF16),
            jax.ShapeDtypeStruct((rows, width), BF16),
            jax.ShapeDtypeStruct((half, rows), BF16),
            jax.ShapeDtypeStruct((3, rows, width), BF16),
            jax.ShapeDtypeStruct((HEADS, rows, rows), F32),
        ],
        in_specs=[smem, smem, whole((1, rows)), codes_spec, scales_spec]
        + [piece_spec] * 4
        + [grad_spec],
        out_specs=[
            term_spec,
            whole((rows, width)),
            whole((half, rows)),
            codes_spec,
            whole((HEADS, rows, rows)),
        ],
        scratch_shapes=[pltpu.VMEM((half, rows), BF16)],
        compiler_params=params,
        cost_estimate=small,
        name="forward",
    )(table, kept_rows, segments, codes, scales, *received, grad_out)
    arrived = lax.ppermute(term_other, "fsdp", swap)
    folded = pl.pallas_call(
        fold_kernel,
        grid=(2,),
        out_shape=jax.ShapeDtypeStruct((half, depth), BF16),
        in_specs=[whole((half, rows)), grad_spec, term_spec],
        out_specs=term_spec,
        compiler_params=light,
        name="fold",
    )(turned_own, grad_out, arrived)
    balanced, folded = lax.optimization_barrier((balanced, folded))
    scattered = lax.psum_scatter(
        folded, "fsdp", scatter_dimension=0, tiled=True, axis_index_groups=cores
    )

    home, *back = pl.pallas_call(
        functools.partial(backward_kernel, group),
        out_shape=[jax.ShapeDtypeStruct((3, rows, width), BF16)] + [piece] * 4,
        in_specs=[
            smem,
            smem,
            whole((width, depth)),
            whole((rows, depth)),
            codes_spec,
            whole((HEADS, rows, rows)),
            scales_spec,
        ],
        out_specs=[codes_spec] + [piece_spec] * 4,
        scratch_shapes=[pltpu.VMEM((rows, width), BF16)],
        compiler_params=params,
        name="backward",
    )(table, kept_rows, w_full, grad_out, balanced, probs, scales)
    chunk = 256
    output = pl.pallas_call(
        output_kernel,
        grid=(depth // chunk,),
        out_shape=jax.ShapeDtypeStruct((rows, depth), BF16),
        in_specs=[whole((rows, width)), pl.BlockSpec((width, chunk), lambda n: (0, n))],
        out_specs=pl.BlockSpec((rows, chunk), lambda n: (0, n)),
        compiler_params=params,
        name="project",
    )(context, w_full)
    returned = [shifted(back[d], "dp", -OFFSETS[d]) for d in range(4)]

    grad_codes = pl.pallas_call(
        return_kernel,
        out_shape=jax.ShapeDtypeStruct((3, rows, width), BF16),
        in_specs=[smem, codes_spec, scales_spec]
        + [piece_spec] * 4
        + [pl.BlockSpec(memory_space=pl.ANY)],
        out_specs=codes_spec,
        compiler_params=params,
        name="restore",
    )(table, home, scales, *returned, output)
    grad_w = pl.pallas_call(
        widen_kernel,
        out_shape=jax.ShapeDtypeStruct(w_out.shape, F32),
        in_specs=[pl.BlockSpec(memory_space=pl.ANY), whole(w_out.shape)],
        out_specs=whole(w_out.shape),
        compiler_params=params,
        name="widen",
    )(grad_codes, scattered)
    grad_codes = jnp.transpose(grad_codes, (1, 0, 2))
    return (output[None, None], grad_codes[None, None], grad_w[None])


def solution(mesh):
    return jax.shard_map(
        local,
        mesh=mesh,
        in_specs=(
            P("dp", "fsdp", None, None, None),
            P("dp", "fsdp", None, None, None),
            P("dp", "fsdp", None),
            P("dp", "fsdp"),
            P(None, "fsdp", None, None),
            P("fsdp", None),
            P("dp", "fsdp", None, None),
        ),
        out_specs=(
            P("dp", "fsdp", None, None),
            P("dp", "fsdp", None, None, None),
            P("dp", "fsdp", None),
        ),
        check_vma=False,
    )
```

```python
import functools
import math

import jax
import jax.numpy as jnp
from jax import lax
from jax.experimental import pallas as pl
from jax.experimental.pallas import tpu as pltpu
from jax.sharding import PartitionSpec as P

HEADS = 8
OFFSETS = (1, -1, 2, -2)
FAR_FIRST = (2, 3, 0, 1)
SLOT = 16
LANES = 128
F32 = jnp.float32
BF16 = jnp.bfloat16
NT = (((1,), (1,)), ((), ()))
TN = (((0,), (0,)), ((), ()))


def shifted(block, axis, distance):
    devices = range(lax.axis_size(axis))
    route = [(i - distance, i) for i in devices if i - distance in devices]
    return lax.ppermute(block, axis, route)


def dot(a, b, dims=(((1,), (0,)), ((), ()))):
    return lax.dot_general(a, b, dims, preferred_element_type=F32)


def sent_spans(table, at):
    return [(table[0, d, at], table[1, d, at]) for d in range(4)]


def placed_spans(table, at, group):
    spans = []
    for d in range(4):
        source = at - OFFSETS[d]
        allowed = (source >= 0) & (source < group)
        source = jnp.clip(source, 0, group - 1)
        spans.append((table[2, d, source], jnp.where(allowed, table[1, d, source], 0)))
    return spans


def one_hot(spans, rows, slots_first):
    shape = (4 * SLOT, rows) if slots_first else (rows, 4 * SLOT)
    slot = lax.broadcasted_iota(jnp.int32, shape, 0 if slots_first else 1)
    row = lax.broadcasted_iota(jnp.int32, shape, 1 if slots_first else 0)
    hot = None
    for d, (first, length) in enumerate(spans):
        i = slot - SLOT * d
        here = (i >= 0) & (i < length) & (row == first + i)
        hot = here if hot is None else hot | here
    return jnp.where(hot, 1.0, 0.0).astype(BF16)


def expanded(select, scales):
    columns = dot(select, scales, NT)
    return jnp.concatenate(
        [
            jnp.broadcast_to(columns[:, b : b + 1], (select.shape[0], LANES))
            for b in range(scales.shape[0])
        ],
        axis=1,
    )


def window(head, size):
    low = head * size // LANES
    high = ((head + 1) * size - 1) // LANES + 1
    return low, high


def head_mask(head, size, rows):
    low, high = window(head, size)
    column = lax.broadcasted_iota(jnp.int32, (rows, (high - low) * LANES), 1) + low * LANES
    return (column >= head * size) & (column < (head + 1) * size)


def add_tiles(tiles, part, low):
    for i in range(part.shape[1] // LANES):
        piece = part[:, i * LANES : (i + 1) * LANES]
        tiles[low + i] = piece if tiles[low + i] is None else tiles[low + i] + piece


def pack_kernel(table, codes, scales, *sent):
    at = lax.axis_index("dp")
    rows = codes.shape[1]
    select = one_hot(sent_spans(table, at), rows, True)
    for c in range(3):
        values = dot(select, codes[c]) * expanded(select, scales[c])
        values = values.astype(BF16)
        for d in range(4):
            sent[d][c] = values[d * SLOT : (d + 1) * SLOT]


def split_order(width, half, core):
    count = width // 2
    part = width // HEADS // 2
    slot = lax.broadcasted_iota(jnp.int32, (1, count), 1)
    chip = jnp.zeros((1, count), jnp.int32)
    for x in range(1, HEADS):
        chip += jnp.where(slot >= x * part, 1, 0)
    side = core if half == 0 else 1 - core
    source = slot + part * chip + part * side
    row = lax.broadcasted_iota(jnp.int32, (width, count), 0)
    return jnp.where(row == source, 1.0, 0.0).astype(BF16)


def forward_kernel(
    group, table, kept, segments, codes, scales, r2, r3, r0, r1, grad_out,
    term_other, context_out, turned_own, balanced, probs_out, turned
):
    rows, width = codes.shape[1:]
    size = width // HEADS
    factor = 1.0 / math.sqrt(size)

    @pl.when(pl.program_id(0) == 0)
    def _():
        at = lax.axis_index("dp")
        core = lax.rem(lax.axis_index("fsdp"), 2)
        keep = kept[0, 0]
        spans = placed_spans(table, at, group)
        place = one_hot(spans, rows, False)
        row = lax.broadcasted_iota(jnp.int32, (rows, rows), 0)
        lane = lax.broadcasted_iota(jnp.int32, (rows, rows), 1)
        eye = row == lane
        identity = jnp.where(eye, 1.0, 0.0).astype(BF16)
        along = jnp.broadcast_to(segments[...], (rows, rows))
        labels = jnp.where(lane < keep, along, -1)
        for d, (first, length) in enumerate(spans):
            labels = jnp.where((lane >= first) & (lane < first + length), 100000 + d, labels)
        labels = labels.astype(F32)
        down = jnp.sum(jnp.where(eye, labels, 0.0), axis=1, keepdims=True)
        same = labels == down
        column_row = lax.broadcasted_iota(jnp.int32, (rows, width), 0)
        for c in range(3):
            own = (codes[c].astype(F32) * expanded(identity, scales[c])).astype(BF16)
            own = jnp.where(column_row < keep, own.astype(F32), 0.0)
            arrived = jnp.concatenate([r0[c], r1[c], r2[c], r3[c]], axis=0)
            balanced[c] = (own + dot(place, arrived)).astype(BF16)
        tiles = [None] * (width // LANES)
        for head in range(HEADS):
            low, high = window(head, size)
            cut = slice(low * LANES, high * LANES)
            mask = head_mask(head, size, rows)
            query = balanced[0, :, cut]
            keys = jnp.where(mask, balanced[1, :, cut].astype(F32), 0.0).astype(BF16)
            values = jnp.where(mask, balanced[2, :, cut].astype(F32), 0.0).astype(BF16)
            scores = jnp.where(same, dot(query, keys, NT) * factor, -jnp.inf)
            weights = jnp.exp(scores - jnp.max(scores, axis=1, keepdims=True))
            probs = weights / jnp.sum(weights, axis=1, keepdims=True)
            probs_out[head] = probs
            add_tiles(tiles, dot(probs.astype(BF16), values), low)
        context = jnp.concatenate(tiles, axis=1).astype(BF16)
        context_out[...] = context
        for half, flipped in enumerate((turned_own, turned)):
            flipped[...] = dot(context, split_order(width, half, core)).T.astype(BF16)

    term_other[...] = dot(turned[...], grad_out[...]).astype(BF16)


def fold_kernel(turned_own, grad_out, arrived, folded):
    own = dot(turned_own[...], grad_out[...]).astype(BF16)
    folded[...] = (own.astype(F32) + arrived[...].astype(F32)).astype(BF16)


def widen_kernel(_, narrow, wide):
    wide[...] = narrow[...].astype(F32)


def output_kernel(context, w, output):
    output[...] = dot(context[...], w[...]).astype(BF16)


def backward_kernel(
    group, table, kept, w, grad_out, balanced, probs_in, scales,
    home, b0, b1, b2, b3, upstream_all
):
    rows, width = balanced.shape[1:]
    size = width // HEADS
    factor = 1.0 / math.sqrt(size)
    upstream_all[...] = dot(grad_out[...], w[...], NT).astype(BF16)
    at = lax.axis_index("dp")
    keep = kept[0, 0]
    grads = [[None] * (width // LANES) for _ in range(3)]
    for head in range(HEADS):
        low, high = window(head, size)
        cut = slice(low * LANES, high * LANES)
        mask = head_mask(head, size, rows)

        def masked(values):
            return jnp.where(mask, values.astype(F32), 0.0).astype(BF16)

        query = masked(balanced[0, :, cut])
        keys = masked(balanced[1, :, cut])
        values = balanced[2, :, cut]
        upstream = masked(upstream_all[:, cut])
        probs = probs_in[head]
        grad_probs = dot(upstream, values, NT)
        total = jnp.sum(probs * grad_probs, axis=1, keepdims=True)
        grad_scores = probs * (grad_probs - total) * factor
        add_tiles(grads[0], dot(grad_scores.astype(BF16), keys), low)
        add_tiles(grads[1], dot(grad_scores.T.astype(BF16), query), low)
        add_tiles(grads[2], dot(probs.T.astype(BF16), upstream), low)
    select = one_hot(placed_spans(table, at, group), rows, True)
    row = lax.broadcasted_iota(jnp.int32, (rows, rows), 0)
    lane = lax.broadcasted_iota(jnp.int32, (rows, rows), 1)
    identity = jnp.where((row == lane) & (row < keep), 1.0, 0.0).astype(BF16)
    for c in range(3):
        grad = jnp.concatenate(grads[c], axis=1)
        home[c] = (grad * expanded(identity, scales[c])).astype(BF16)
        back = dot(select, grad.astype(BF16)).astype(BF16)
        for d, ref in enumerate((b0, b1, b2, b3)):
            ref[c] = back[d * SLOT : (d + 1) * SLOT]


def return_kernel(table, home, scales, r2, r3, r0, r1, _, grad_codes):
    at = lax.axis_index("dp")
    rows = home.shape[1]
    place = one_hot(sent_spans(table, at), rows, False)
    row = lax.broadcasted_iota(jnp.int32, (rows, rows), 0)
    lane = lax.broadcasted_iota(jnp.int32, (rows, rows), 1)
    identity = jnp.where(row == lane, 1.0, 0.0).astype(BF16)
    for c in range(3):
        arrived = jnp.concatenate([r0[c], r1[c], r2[c], r3[c]], axis=0)
        moved = dot(place, arrived) * expanded(identity, scales[c])
        grad_codes[c] = (home[c].astype(F32) + moved).astype(BF16)


def whole(shape):
    return pl.BlockSpec(shape, lambda *_: (0,) * len(shape))


def local(qkv_codes, block_scales, home_segments, kept_rows, pack_list, w_out, cotangent):
    group = lax.axis_size("dp")
    codes = jnp.transpose(qkv_codes[0, 0], (1, 0, 2))
    scales = jnp.transpose(block_scales[0, 0], (1, 2, 0))
    segments = home_segments[0]
    table = jnp.transpose(pack_list[:, 0], (2, 1, 0))
    grad_out = cotangent[0, 0]
    _, rows, width = codes.shape
    depth = w_out.shape[1]
    blocks = scales.shape[1]
    devices = lax.axis_size("fsdp")
    half = width // 2
    cores = [list(range(core, devices, 2)) for core in range(2)]
    swap = [(i, i + 1 - 2 * (i % 2)) for i in range(devices)]
    smem = pl.BlockSpec(memory_space=pltpu.SMEM)
    params = pltpu.CompilerParams(vmem_limit_bytes=56 * 1024 * 1024)
    light = pltpu.CompilerParams(vmem_limit_bytes=24 * 1024 * 1024)
    small = pl.CostEstimate(flops=1, bytes_accessed=1, transcendentals=0)
    piece = jax.ShapeDtypeStruct((3, SLOT, width), BF16)
    piece_spec = whole((3, SLOT, width))
    codes_spec = whole((3, rows, width))
    scales_spec = whole((3, blocks, rows))

    w_full = lax.all_gather(w_out, "fsdp", axis=0, tiled=True)

    sent = pl.pallas_call(
        pack_kernel,
        out_shape=[piece] * 4,
        in_specs=[smem, codes_spec, scales_spec],
        out_specs=[piece_spec] * 4,
        compiler_params=params,
        cost_estimate=small,
        name="pack",
    )(table, codes, scales)
    received = [shifted(sent[d], "dp", OFFSETS[d]) for d in FAR_FIRST]

    span = depth // 2
    term_spec = pl.BlockSpec((half, span), lambda n: (0, n))
    grad_spec = pl.BlockSpec((rows, span), lambda n: (0, n))
    term_other, context, turned_own, balanced, probs = pl.pallas_call(
        functools.partial(forward_kernel, group),
        grid=(2,),
        out_shape=[
            jax.ShapeDtypeStruct((half, depth), BF16),
            jax.ShapeDtypeStruct((rows, width), BF16),
            jax.ShapeDtypeStruct((half, rows), BF16),
            jax.ShapeDtypeStruct((3, rows, width), BF16),
            jax.ShapeDtypeStruct((HEADS, rows, rows), F32),
        ],
        in_specs=[smem, smem, whole((1, rows)), codes_spec, scales_spec]
        + [piece_spec] * 4
        + [grad_spec],
        out_specs=[
            term_spec,
            whole((rows, width)),
            whole((half, rows)),
            codes_spec,
            whole((HEADS, rows, rows)),
        ],
        scratch_shapes=[pltpu.VMEM((half, rows), BF16)],
        compiler_params=params,
        cost_estimate=small,
        name="forward",
    )(table, kept_rows, segments, codes, scales, *received, grad_out)
    arrived = lax.ppermute(term_other, "fsdp", swap)
    folded = pl.pallas_call(
        fold_kernel,
        grid=(2,),
        out_shape=jax.ShapeDtypeStruct((half, depth), BF16),
        in_specs=[whole((half, rows)), grad_spec, term_spec],
        out_specs=term_spec,
        compiler_params=light,
        name="fold",
    )(turned_own, grad_out, arrived)
    balanced, folded = lax.optimization_barrier((balanced, folded))
    scattered = lax.psum_scatter(
        folded, "fsdp", scatter_dimension=0, tiled=True, axis_index_groups=cores
    )

    home, *back = pl.pallas_call(
        functools.partial(backward_kernel, group),
        out_shape=[jax.ShapeDtypeStruct((3, rows, width), BF16)] + [piece] * 4,
        in_specs=[
            smem,
            smem,
            whole((width, depth)),
            whole((rows, depth)),
            codes_spec,
            whole((HEADS, rows, rows)),
            scales_spec,
        ],
        out_specs=[codes_spec] + [piece_spec] * 4,
        scratch_shapes=[pltpu.VMEM((rows, width), BF16)],
        compiler_params=params,
        name="backward",
    )(table, kept_rows, w_full, grad_out, balanced, probs, scales)
    chunk = 256
    output = pl.pallas_call(
        output_kernel,
        grid=(depth // chunk,),
        out_shape=jax.ShapeDtypeStruct((rows, depth), BF16),
        in_specs=[whole((rows, width)), pl.BlockSpec((width, chunk), lambda n: (0, n))],
        out_specs=pl.BlockSpec((rows, chunk), lambda n: (0, n)),
        compiler_params=params,
        name="project",
    )(context, w_full)
    returned = [shifted(back[d], "dp", -OFFSETS[d]) for d in FAR_FIRST]

    grad_codes = pl.pallas_call(
        return_kernel,
        out_shape=jax.ShapeDtypeStruct((3, rows, width), BF16),
        in_specs=[smem, codes_spec, scales_spec]
        + [piece_spec] * 4
        + [pl.BlockSpec(memory_space=pl.ANY)],
        out_specs=codes_spec,
        compiler_params=params,
        name="restore",
    )(table, home, scales, *returned, output)
    grad_w = pl.pallas_call(
        widen_kernel,
        out_shape=jax.ShapeDtypeStruct(w_out.shape, F32),
        in_specs=[pl.BlockSpec(memory_space=pl.ANY), whole(w_out.shape)],
        out_specs=whole(w_out.shape),
        compiler_params=params,
        name="widen",
    )(grad_codes, scattered)
    grad_codes = jnp.transpose(grad_codes, (1, 0, 2))
    return (output[None, None], grad_codes[None, None], grad_w[None])


def solution(mesh):
    return jax.shard_map(
        local,
        mesh=mesh,
        in_specs=(
            P("dp", "fsdp", None, None, None),
            P("dp", "fsdp", None, None, None),
            P("dp", "fsdp", None),
            P("dp", "fsdp"),
            P(None, "fsdp", None, None),
            P("fsdp", None),
            P("dp", "fsdp", None, None),
        ),
        out_specs=(
            P("dp", "fsdp", None, None),
            P("dp", "fsdp", None, None, None),
            P("dp", "fsdp", None),
        ),
        check_vma=False,
    )
```
